32 devices in a mesh: rad: 8 (over y, x, core), azi: 4 (over z).
Axes of the slice: x: 2, y: 2, z: 4, core: 2. Of those that a mesh axis runs over, the one named last changes fastest.
Arguments:
- fields: float32 [5, 256, 64, 128], P(None, 'rad', 'azi'), may hold values from -6 to 6
- kappa: float32 [256, 64, 128], P('rad', 'azi'), may hold values from 0.01 to 0.1
- radial_speed: float32 [5, 256], P(None, 'rad'), may hold values from -0.5 to 0.5
- azimuth_speed: float32 [5, 256], P(None, 'rad'), may hold values from -0.5 to 0.5
- shifts: int32 [256], P('rad'), may hold values from 0 to 63
Outputs:
- advanced: float32 [5, 256, 64, 128], P(None, 'rad', 'azi')
The draws below stay inside these ranges and needn't reach their ends.
All inputs are finite; a program needn't handle non-finite values.
Results may differ from the reference program's by a relative error of at most 0.00002.
Values sent between devices are 32-bit elements; how exact they have to be, the bound alone decides.
A program may use at most 64 MiB of HBM per device.

```python
import math
import jax
import jax.numpy as jnp
from jax import lax

F = 5
NZ = 128
NR = 256
NA = 64


def with_ends(values, key, low, top_value):
    longest = values.shape.index(max(values.shape))
    spots = []
    for shift in (0, 1):
        where = [jax.random.randint(jax.random.fold_in(key, axis), (), 0, length) for axis, length in enumerate(values.shape)]
        where[longest] = (where[longest] + shift) % values.shape[longest]
        spots.append(tuple(where))
    return values.at[spots[0]].set(low).at[spots[1]].set(top_value)


def level_of(own_key, extent, pieces, low, high):
    factor_of, own = 1.0, jax.random.fold_in(own_key, 6)
    for position, parts in pieces:
        steps = jnp.exp(jax.random.uniform(jax.random.fold_in(own, position), (parts,), jnp.float32, low / len(pieces), high / len(pieces)))
        factor_of = factor_of * jnp.repeat(steps, extent[position] // parts).reshape([-1 if axis == position else 1 for axis in range(len(extent))])
    return factor_of


def normal_values(rng, extent, scale, limit, cuts=(), kind=jnp.bfloat16):
    factor_of = level_of(rng, extent, cuts, -0.22, 0.18) if cuts else 1.0
    result = jax.random.normal(rng, extent, jnp.float32) * scale * factor_of
    return jnp.minimum(jnp.maximum(result, -limit), limit).astype(kind)


def setup_inputs(seed: int = 0) -> dict:
    key_list = jax.random.split(jax.random.key(seed), 6)
    fields = normal_values(key_list[0], (F, NR, NA, NZ), 1.0, 6.0, ((1, 8), (2, 4)), jnp.float32)
    kappa = jnp.clip(jnp.exp(math.log(0.1) - 2.3025851 * jax.random.uniform(key_list[1], (NR, NA, NZ), jnp.float32) ** level_of(key_list[1], (NR, NA, NZ), ((0, 8), (1, 4)), -0.2, 0.2)), 0.01, 0.1)
    radial_speed = jnp.clip(jax.random.uniform(key_list[2], (F, NR), jnp.float32, -0.5, 0.5) * level_of(key_list[2], (F, NR), ((1, 8),), -0.4, 0.0), -0.5, 0.5)
    azimuth_speed = jnp.clip(jax.random.uniform(key_list[3], (F, NR), jnp.float32, -0.5, 0.5) * level_of(key_list[3], (F, NR), ((1, 8),), -0.4, 0.0), -0.5, 0.5)
    shifts = with_ends(jax.random.randint(key_list[4], (NR,), 0, NA), jax.random.fold_in(key_list[4], 1), 0, NA - 1).astype(jnp.int32)
    return dict(fields=fields, kappa=kappa, radial_speed=radial_speed, azimuth_speed=azimuth_speed, shifts=shifts)


def stencil(padded, kap, speed_r, speed_p):
    n_r = padded.shape[1] - 4
    n_p = padded.shape[2] - 4

    def tap(a, b):
        return padded[:, 2 + a:2 + a + n_r, 2 + b:2 + b + n_p, :]

    centre = tap(0, 0)
    height = centre.shape[3]
    zpad = jnp.pad(centre, ((0, 0), (0, 0), (0, 0), (2, 2)))

    def ztap(a):
        return zpad[:, :, :, 2 + a:2 + a + height]

    first_r = (tap(-2, 0) - 8.0 * tap(-1, 0) + 8.0 * tap(1, 0) - tap(2, 0)) / 12.0
    first_p = (tap(0, -2) - 8.0 * tap(0, -1) + 8.0 * tap(0, 1) - tap(0, 2)) / 12.0
    second_r = (-tap(-2, 0) + 16.0 * tap(-1, 0) - 30.0 * centre + 16.0 * tap(1, 0) - tap(2, 0)) / 12.0
    second_p = (-tap(0, -2) + 16.0 * tap(0, -1) - 30.0 * centre + 16.0 * tap(0, 1) - tap(0, 2)) / 12.0
    second_z = (-ztap(-2) + 16.0 * ztap(-1) - 30.0 * centre + 16.0 * ztap(1) - ztap(2)) / 12.0
    return (-speed_r[:, :, None, None] * first_r - speed_p[:, :, None, None] * first_p
            + kap[None] * (second_r + second_p + second_z))


def operate(field, kap, speed_r, speed_p):
    padded = jnp.pad(field, ((0, 0), (2, 2), (0, 0), (0, 0)))
    padded = jnp.concatenate([padded[:, :, -2:], padded, padded[:, :, :2]], axis=2)
    return stencil(padded, kap, speed_r, speed_p)


def heun(field, kap, speed_r, speed_p):
    first = field + operate(field, kap, speed_r, speed_p)
    return 0.5 * (field + first + operate(first, kap, speed_r, speed_p))


def one_field(items, kappa, shifts):
    field, speed_r, speed_p = items
    field = field[None]
    speed_r = speed_r[None]
    speed_p = speed_p[None]
    half = heun(field, kappa, speed_r, speed_p)
    count = half.shape[2]
    index = (jnp.arange(count, dtype=jnp.int32)[None, :] - shifts[:, None]) % count
    index = jnp.broadcast_to(index[None, :, :, None], half.shape).astype(jnp.int32)
    moved = jnp.take_along_axis(half, index, axis=2)
    return heun(moved, kappa, speed_r, speed_p)[0]


def reference(fields, kappa, radial_speed, azimuth_speed, shifts):
    return lax.map(lambda items: one_field(items, kappa, shifts), (fields, radial_speed, azimuth_speed))
```

```python
import functools

import jax
import jax.numpy as jnp
from jax import lax
from jax.experimental import pallas as pl
from jax.experimental.pallas import tpu as pltpu
from jax.sharding import PartitionSpec as P

MESH = pl.DeviceIdType.MESH
STAGES = 4
AHEAD = 2


def block_of(rad, azi, n):
    column = rad // 2
    odd = lax.rem(column, 2)
    place = azi + odd * (n - 1 - 2 * azi)
    return column * (2 * n) + 2 * place + lax.rem(rad, 2)


def owner_of(block, n):
    column = block // (2 * n)
    t = lax.rem(block, 2 * n)
    odd = lax.rem(column, 2)
    place = t // 2
    return 2 * column + lax.rem(t, 2), place + odd * (n - 1 - 2 * place)


def kernel(n, blocks, srad, sazi, shifts, fields, kappa, out, x0, x1, x2, x3, adv, kap,
           send1, recv1, send_h, recv_h, send2, recv2):
    count, rows, width = fields.shape[0], fields.shape[1], fields.shape[2]
    own = rows // n
    around = width * n
    depth = fields.shape[3]
    rad, azi = lax.axis_index("rad"), lax.axis_index("azi")
    mine = block_of(rad, azi, n)
    home = mine // n
    spot = lax.rem(mine, n)
    has_prev, has_next = mine > 0, mine < blocks - 1
    prev = owner_of(jnp.maximum(mine - 1, 0), n)
    following = owner_of(jnp.minimum(mine + 1, blocks - 1), n)
    targets = [owner_of(rad * n + b, n) for b in range(n)]
    same = [jnp.logical_and(d[0] == rad, d[1] == azi) for d in targets]
    sources = [(home, jnp.int32(a)) for a in range(n)]
    back = [jnp.logical_and(home == rad, azi == a) for a in range(n)]

    barrier = pltpu.get_barrier_semaphore()
    greeted = jnp.int32(0)
    for device, skip in [*zip(targets, same), *zip(sources, back),
                         (prev, jnp.logical_not(has_prev)), (following, jnp.logical_not(has_next))]:
        @pl.when(jnp.logical_not(skip))
        def _():
            pl.semaphore_signal(barrier, inc=1, device_id=device, device_id_type=MESH)
        greeted = greeted + jnp.where(skip, 0, 1)
    pl.semaphore_wait(barrier, greeted)

    def first_pass(f, act):
        for b in range(n):
            def parts():
                at = pl.ds(azi * width, width)
                if f is None:
                    return kappa.at[pl.ds(b * own, own)], kap.at[:, at], count
                return fields.at[f, pl.ds(b * own, own)], x0.at[f, pl.ds(2, own), at], f

            @pl.when(jnp.logical_not(same[b]))
            def _():
                src, dst, k = parts()
                copy = pltpu.make_async_remote_copy(
                    src, dst, send1.at[k, b], recv1.at[k], device_id=targets[b], device_id_type=MESH)
                copy.start() if act == "start" else copy.wait_send()

            if act == "start":
                @pl.when(same[b])
                def _():
                    src, dst, k = parts()
                    pltpu.make_async_copy(src, dst, recv1.at[k]).start()

    def second_pass(f, act):
        for a in range(n):
            def parts():
                return adv.at[f, :, pl.ds(a * width, width)], out.at[f, pl.ds(spot * own, own)]

            @pl.when(jnp.logical_not(back[a]))
            def _():
                src, dst = parts()
                copy = pltpu.make_async_remote_copy(
                    src, dst, send2.at[f, a], recv2.at[f], device_id=sources[a], device_id_type=MESH)
                copy.start() if act == "start" else copy.wait_send()

            if act == "start":
                @pl.when(back[a])
                def _():
                    src, dst = parts()
                    pltpu.make_async_copy(src, dst, recv2.at[f]).start()

    def halo(x, f, level, act):
        low = pltpu.make_async_remote_copy(
            x.at[f, pl.ds(2, 2)], x.at[f, pl.ds(own + 2, 2)], send_h.at[f, level, 0],
            recv_h.at[f, level, 0], device_id=prev, device_id_type=MESH)
        high = pltpu.make_async_remote_copy(
            x.at[f, pl.ds(own, 2)], x.at[f, pl.ds(0, 2)], send_h.at[f, level, 1],
            recv_h.at[f, level, 1], device_id=following, device_id_type=MESH)

        @pl.when(has_prev)
        def _():
            if act == "start":
                low.start()
            elif act == "send":
                low.wait_send()
            else:
                high.wait_recv()

        @pl.when(has_next)
        def _():
            if act == "start":
                high.start()
            elif act == "send":
                high.wait_send()
            else:
                low.wait_recv()

    lane = lax.broadcasted_iota(jnp.int32, (around, depth), 1)

    def operate(x, f, i):
        u = x[f, i + 2]
        r2m, r1m, r1p, r2p = x[f, i], x[f, i + 1], x[f, i + 3], x[f, i + 4]
        p1p, p1m = pltpu.roll(u, around - 1, 0), pltpu.roll(u, 1, 0)
        p2p, p2m = pltpu.roll(u, around - 2, 0), pltpu.roll(u, 2, 0)
        z1p = jnp.where(lane < depth - 1, pltpu.roll(u, depth - 1, 1), 0.0)
        z1m = jnp.where(lane >= 1, pltpu.roll(u, 1, 1), 0.0)
        z2p = jnp.where(lane < depth - 2, pltpu.roll(u, depth - 2, 1), 0.0)
        z2m = jnp.where(lane >= 2, pltpu.roll(u, 2, 1), 0.0)
        one = (r1p + r1m) + (p1p + p1m) + (z1p + z1m)
        two = (r2p + r2m) + (p2p + p2m) + (z2p + z2m)
        spread = 16.0 * one - two - 90.0 * u
        carried = (srad[f, i] * (8.0 * (r1p - r1m) - (r2p - r2m))
                   + sazi[f, i] * (8.0 * (p1p - p1m) - (p2p - p2m)))
        return u, kap[i] * spread - carried

    def each_row(body):
        def step(i, carry):
            body(i)
            return carry
        lax.fori_loop(0, own, step, 0)

    def clear(f, carry):
        for x in (x0, x1, x2, x3):
            @pl.when(jnp.logical_not(has_prev))
            def _():
                x[f, pl.ds(0, 2)] = jnp.zeros((2, around, depth), jnp.float32)

            @pl.when(jnp.logical_not(has_next))
            def _():
                x[f, pl.ds(own + 2, 2)] = jnp.zeros((2, around, depth), jnp.float32)
        return carry

    first_pass(0, "start")
    first_pass(None, "start")
    for f in range(1, min(AHEAD, count)):
        first_pass(f, "start")
    lax.fori_loop(0, count, clear, 0)
    pltpu.make_async_copy(kap, kap, recv1.at[count]).wait()

    def scale(i):
        kap[i] = kap[i] * (1.0 / 12.0)
    each_row(scale)

    def tick(t, carry):
        def at_stage(lag):
            f = t - lag
            return f, jnp.logical_and(f >= 0, f < count)

        f_next, fine = at_stage(-AHEAD)

        @pl.when(fine)
        def _():
            first_pass(f_next, "start")

        f4, fine4 = at_stage(4)

        @pl.when(fine4)
        def _():
            halo(x3, f4, 3, "recv")

            def body(i):
                u, change = operate(x3, f4, i)
                adv[f4, i] = 0.5 * (x2[f4, i + 2] + u + change)
            each_row(body)
            second_pass(f4, "start")

        f3, fine3 = at_stage(3)

        @pl.when(fine3)
        def _():
            halo(x2, f3, 2, "recv")

            def body(i):
                u, change = operate(x2, f3, i)
                x3[f3, i + 2] = u + change
            each_row(body)
            halo(x3, f3, 3, "start")

        f2, fine2 = at_stage(2)

        @pl.when(fine2)
        def _():
            halo(x1, f2, 1, "recv")

            def body(i):
                u, change = operate(x1, f2, i)
                half = 0.5 * (x0[f2, i + 2] + u + change)
                x2[f2, i + 2] = pltpu.roll(half, shifts[i], 0)
            each_row(body)
            halo(x2, f2, 2, "start")

        f1, fine1 = at_stage(1)

        @pl.when(fine1)
        def _():
            halo(x0, f1, 0, "recv")

            def body(i):
                u, change = operate(x0, f1, i)
                x1[f1, i + 2] = u + change
            each_row(body)
            halo(x1, f1, 1, "start")

        f0, fine0 = at_stage(0)

        @pl.when(fine0)
        def _():
            here = x0.at[f0, pl.ds(2, own)]
            pltpu.make_async_copy(here, here, recv1.at[f0]).wait()
            halo(x0, f0, 0, "start")
        return carry

    lax.fori_loop(0, count + STAGES, tick, 0)

    first_pass(None, "send")

    def finish(f, carry):
        first_pass(f, "send")
        for level, x in enumerate((x0, x1, x2, x3)):
            halo(x, f, level, "send")
        second_pass(f, "send")
        pltpu.make_async_copy(out.at[f], out.at[f], recv2.at[f]).wait()
        return carry
    lax.fori_loop(0, count, finish, 0)


def shards(fields, kappa, radial_speed, azimuth_speed, shifts):
    n = lax.axis_size("azi")
    annuli = lax.axis_size("rad")
    count, rows, width, depth = fields.shape
    own, around = rows // n, width * n
    rad, azi = lax.axis_index("rad"), lax.axis_index("azi")
    mine = block_of(rad, azi, n)
    packed = jnp.concatenate(
        [radial_speed * (1.0 / 12.0), azimuth_speed * (1.0 / 12.0),
         jnp.mod(shifts, around).astype(jnp.float32)[None]], axis=0)
    other = lax.ppermute(packed, "rad", [(i, i ^ 1) for i in range(annuli)])
    rightful = jnp.where(mine // n == rad, packed, other)
    rightful = lax.dynamic_slice_in_dim(rightful, (mine % n) * own, own, axis=1)
    srad, sazi = rightful[:count], rightful[count:2 * count]
    turn = rightful[2 * count].astype(jnp.int32)

    tall = pltpu.VMEM((count, own + 4, around, depth), jnp.float32)
    held = 4 * count * around * depth * (4 * (own + 4) + own + own)
    any_space = pl.BlockSpec(memory_space=pl.ANY)
    small = pl.BlockSpec(memory_space=pltpu.SMEM)
    return pl.pallas_call(
        functools.partial(kernel, n, n * annuli),
        out_shape=jax.ShapeDtypeStruct(fields.shape, jnp.float32),
        in_specs=[small, small, small, any_space, any_space],
        out_specs=any_space,
        scratch_shapes=[
            tall, tall, tall, tall,
            pltpu.VMEM((count, own, around, depth), jnp.float32),
            pltpu.VMEM((own, around, depth), jnp.float32),
            pltpu.SemaphoreType.DMA((count + 1, n)),
            pltpu.SemaphoreType.DMA((count + 1,)),
            pltpu.SemaphoreType.DMA((count, STAGES, 2)),
            pltpu.SemaphoreType.DMA((count, STAGES, 2)),
            pltpu.SemaphoreType.DMA((count, n)),
            pltpu.SemaphoreType.DMA((count,)),
        ],
        compiler_params=pltpu.CompilerParams(
            collective_id=0, has_side_effects=True, vmem_limit_bytes=held + (8 << 20)),
    )(srad, sazi, turn, fields, kappa)


def solution(mesh):
    placed = (
        P(None, "rad", "azi", None),
        P("rad", "azi", None),
        P(None, "rad"),
        P(None, "rad"),
        P("rad"),
    )
    return jax.shard_map(
        shards, mesh=mesh, in_specs=placed, out_specs=P(None, "rad", "azi", None), check_vma=False
    )
```

```python
import functools

import jax
import jax.numpy as jnp
from jax import lax
from jax.experimental import pallas as pl
from jax.experimental.pallas import tpu as pltpu
from jax.sharding import PartitionSpec as P

MESH = pl.DeviceIdType.MESH
HALO = 8
STAGES = 4
AHEAD = 2


def block_of(rad, azi, n):
    column = rad // 2
    odd = lax.rem(column, 2)
    place = azi + odd * (n - 1 - 2 * azi)
    return column * (2 * n) + 2 * place + lax.rem(rad, 2)


def owner_of(block, n):
    column = block // (2 * n)
    t = lax.rem(block, 2 * n)
    odd = lax.rem(column, 2)
    place = t // 2
    return 2 * column + lax.rem(t, 2), place + odd * (n - 1 - 2 * place)


def kernel(n, blocks, srad, sazi, shifts, fields, kappa, out, x0, x1, x2, x3, adv, kap,
           send1, recv1, send_x, recv_x, send_h, recv_h, send2, recv2):
    count, rows, width, depth = fields.shape
    own = rows // n
    around = width * n
    rad, azi = lax.axis_index("rad"), lax.axis_index("azi")
    core = lax.rem(rad, 2)
    mine = block_of(rad, azi, n)
    home = mine // n
    spot = lax.rem(mine, n)
    turn = lax.rem(mine, 2 * n)
    middle = jnp.logical_or(turn == n, turn == n - 1)
    has_prev, has_next = mine > 0, mine < blocks - 1
    from_prev = jnp.logical_and(has_prev, turn != n)
    from_next = jnp.logical_and(has_next, turn != n - 1)
    prev = owner_of(jnp.maximum(mine - 1, 0), n)
    following = owner_of(jnp.minimum(mine + 1, blocks - 1), n)

    def is_me(device):
        return jnp.logical_and(device[0] == rad, device[1] == azi)

    targets = [owner_of(rad * n + b, n) for b in range(n)]
    same = [is_me(d) for d in targets]
    sources = [(home, jnp.int32(a)) for a in range(n)]
    back = [is_me(d) for d in sources]
    across = owner_of(rad * n + n - core * (n + 1), n)
    across_same = is_me(across)
    holders = [(home + 1 - 2 * lax.rem(home, 2), jnp.int32(a)) for a in range(n)]
    not_held = [jnp.logical_or(jnp.logical_not(middle), is_me(d)) for d in holders]

    barrier = pltpu.get_barrier_semaphore()
    greeted = jnp.int32(0)
    for device, skip in [*zip(targets, same), *zip(sources, back), (across, across_same),
                         *zip(holders, not_held), (prev, jnp.logical_not(from_prev)),
                         (following, jnp.logical_not(from_next))]:
        @pl.when(jnp.logical_not(skip))
        def _():
            pl.semaphore_signal(barrier, inc=1, device_id=device, device_id_type=MESH)
        greeted = greeted + jnp.where(skip, 0, 1)
    pl.semaphore_wait(barrier, greeted)

    def move(act, src, dst, send, recv, device, local):
        @pl.when(jnp.logical_not(local))
        def _():
            copy = pltpu.make_async_remote_copy(
                src, dst, send, recv, device_id=device, device_id_type=MESH)
            copy.start() if act == "start" else copy.wait_send()

        if act == "start":
            @pl.when(local)
            def _():
                pltpu.make_async_copy(src, dst, recv).start()

    def held(q):
        return kappa if isinstance(q, int) else fields.at[q - 1]

    def first_pass(q, act):
        at = pl.ds(azi * width, width)
        edge = (1 - core) * (rows - HALO)
        move(act, held(q).at[pl.ds(edge, HALO)], x0.at[q, pl.ds(core * (HALO + own), HALO), at],
             send_x.at[q], recv_x.at[q], across, across_same)
        for b in range(n):
            move(act, held(q).at[pl.ds(b * own, own)], x0.at[q, pl.ds(HALO, own), at],
                 send1.at[q, b], recv1.at[q], targets[b], same[b])

    def second_pass(f, act):
        for a in range(n):
            move(act, adv.at[f, :, pl.ds(a * width, width)], out.at[f, pl.ds(spot * own, own)],
                 send2.at[f, a], recv2.at[f], sources[a], back[a])

    def halo(q, act):
        low = pltpu.make_async_remote_copy(
            x0.at[q, pl.ds(HALO, HALO)], x0.at[q, pl.ds(own + HALO, HALO)], send_h.at[q, 0],
            recv_h.at[q, 0], device_id=prev, device_id_type=MESH)
        high = pltpu.make_async_remote_copy(
            x0.at[q, pl.ds(own, HALO)], x0.at[q, pl.ds(0, HALO)], send_h.at[q, 1],
            recv_h.at[q, 1], device_id=following, device_id_type=MESH)

        @pl.when(from_prev)
        def _():
            if act == "start":
                low.start()
            elif act == "send":
                low.wait_send()
            else:
                high.wait_recv()

        @pl.when(from_next)
        def _():
            if act == "start":
                high.start()
            elif act == "send":
                high.wait_send()
            else:
                low.wait_recv()

        if act == "recv":
            @pl.when(middle)
            def _():
                here = x0.at[q, pl.ds(0, HALO)]
                pltpu.make_async_copy(here, here, recv_x.at[q]).wait()

    lane = lax.broadcasted_iota(jnp.int32, (around, depth), 1)

    def operate(x, f, i, row):
        u = x[i + 2]
        r2m, r1m, r1p, r2p = x[i], x[i + 1], x[i + 3], x[i + 4]
        p1p, p1m = pltpu.roll(u, around - 1, 0), pltpu.roll(u, 1, 0)
        p2p, p2m = pltpu.roll(u, around - 2, 0), pltpu.roll(u, 2, 0)
        z1p = jnp.where(lane < depth - 1, pltpu.roll(u, depth - 1, 1), 0.0)
        z1m = jnp.where(lane >= 1, pltpu.roll(u, 1, 1), 0.0)
        z2p = jnp.where(lane < depth - 2, pltpu.roll(u, depth - 2, 1), 0.0)
        z2m = jnp.where(lane >= 2, pltpu.roll(u, 2, 1), 0.0)
        one = (r1p + r1m) + (p1p + p1m) + (z1p + z1m)
        two = (r2p + r2m) + (p2p + p2m) + (z2p + z2m)
        spread = 16.0 * one - two - 90.0 * u
        carried = (srad[f, row] * (8.0 * (r1p - r1m) - (r2p - r2m))
                   + sazi[f, row] * (8.0 * (p1p - p1m) - (p2p - p2m)))
        return u, kap[row] * spread - carried

    def each_row(length, body):
        def step(i, carry):
            body(i)
            return carry
        lax.fori_loop(0, length, step, 0)

    def clear(q, carry):
        @pl.when(jnp.logical_not(has_prev))
        def _():
            x0[q, pl.ds(0, HALO)] = jnp.zeros((HALO, around, depth), jnp.float32)

        @pl.when(jnp.logical_not(has_next))
        def _():
            x0[q, pl.ds(own + HALO, HALO)] = jnp.zeros((HALO, around, depth), jnp.float32)
        return carry

    def pass_on(q):
        here = x0.at[q, pl.ds(HALO, own)]
        pltpu.make_async_copy(here, here, recv1.at[q]).wait()
        halo(q, "start")

    def begin(q, carry):
        first_pass(q, "start")
        return carry

    first_pass(0, "start")
    lax.fori_loop(1, count + 1, begin, 0)
    lax.fori_loop(0, count + 1, clear, 0)
    pass_on(0)
    halo(0, "recv")

    def scale(i):
        kap[i] = x0[0, i] * (1.0 / 12.0)
    each_row(own + 2 * HALO, scale)

    def tick(t, carry):
        @pl.when(t <= count)
        def _():
            pass_on(t)

        @pl.when(t >= 2)
        def _():
            q = t - 1
            f = q - 1
            halo(q, "recv")
            base = x0.at[q]

            def body1(i):
                u, change = operate(base, f, i, i + 2)
                x1[i] = u + change
            each_row(own + 2 * HALO - 4, body1)

            def body2(i):
                u, change = operate(x1, f, i, i + 4)
                half = 0.5 * (base[i + 4] + u + change)
                x2[i] = pltpu.roll(half, shifts[i + 4], 0)
            each_row(own + 2 * HALO - 8, body2)

            def body3(i):
                u, change = operate(x2, f, i, i + 6)
                x3[i] = u + change
            each_row(own + 2 * HALO - 12, body3)

            def body4(i):
                u, change = operate(x3, f, i, i + 8)
                adv[f, i] = 0.5 * (x2[i + 4] + u + change)
            each_row(own, body4)
            second_pass(f, "start")
        return carry

    lax.fori_loop(1, count + 2, tick, 0)

    first_pass(0, "send")
    halo(0, "send")

    def finish(f, carry):
        first_pass(f + 1, "send")
        halo(f + 1, "send")
        second_pass(f, "send")
        pltpu.make_async_copy(out.at[f], out.at[f], recv2.at[f]).wait()
        return carry
    lax.fori_loop(0, count, finish, 0)


def shards(fields, kappa, radial_speed, azimuth_speed, shifts):
    n = lax.axis_size("azi")
    annuli = lax.axis_size("rad")
    count, rows, width, depth = fields.shape
    own, around = rows // n, width * n
    if own < HALO or n % 2:
        return shards_by_steps(fields, kappa, radial_speed, azimuth_speed, shifts)
    rad, azi = lax.axis_index("rad"), lax.axis_index("azi")
    mine = block_of(rad, azi, n)
    packed = jnp.concatenate(
        [radial_speed * (1.0 / 12.0), azimuth_speed * (1.0 / 12.0),
         jnp.mod(shifts, around).astype(jnp.float32)[None]], axis=0)
    below = lax.ppermute(packed, "rad", [(i, i + 1) for i in range(annuli - 1)])
    above = lax.ppermute(packed, "rad", [(i + 1, i) for i in range(annuli - 1)])
    wide = jnp.concatenate([below, packed, above], axis=1)
    start = mine * own - HALO - (rad - 1) * rows
    tall = own + 2 * HALO
    wide = lax.dynamic_slice_in_dim(wide, start, tall, axis=1)
    srad, sazi = wide[:count], wide[count:2 * count]
    turn = wide[2 * count].astype(jnp.int32)

    def scratch(*lead):
        return pltpu.VMEM((*lead, around, depth), jnp.float32)

    held = 4 * around * depth * ((count + 2) * tall + 3 * tall + count * own)
    any_space = pl.BlockSpec(memory_space=pl.ANY)
    small = pl.BlockSpec(memory_space=pltpu.SMEM)
    dma = pltpu.SemaphoreType.DMA
    return pl.pallas_call(
        functools.partial(kernel, n, n * annuli),
        out_shape=jax.ShapeDtypeStruct(fields.shape, jnp.float32),
        in_specs=[small, small, small, any_space, any_space],
        out_specs=any_space,
        scratch_shapes=[
            scratch(count + 1, tall), scratch(tall - 4), scratch(tall - 8), scratch(tall - 12),
            scratch(count, own), scratch(tall),
            dma((count + 1, n)), dma((count + 1,)), dma((count + 1,)), dma((count + 1,)),
            dma((count + 1, 2)), dma((count + 1, 2)), dma((count, n)), dma((count,)),
        ],
        compiler_params=pltpu.CompilerParams(
            collective_id=0, has_side_effects=True, vmem_limit_bytes=held + (8 << 20)),
    )(srad, sazi, turn, fields, kappa)


def kernel_by_steps(n, blocks, srad, sazi, shifts, fields, kappa, out, x0, x1, x2, x3, adv, kap,
           send1, recv1, send_h, recv_h, send2, recv2):
    count, rows, width = fields.shape[0], fields.shape[1], fields.shape[2]
    own = rows // n
    around = width * n
    depth = fields.shape[3]
    rad, azi = lax.axis_index("rad"), lax.axis_index("azi")
    mine = block_of(rad, azi, n)
    home = mine // n
    spot = lax.rem(mine, n)
    has_prev, has_next = mine > 0, mine < blocks - 1
    prev = owner_of(jnp.maximum(mine - 1, 0), n)
    following = owner_of(jnp.minimum(mine + 1, blocks - 1), n)
    targets = [owner_of(rad * n + b, n) for b in range(n)]
    same = [jnp.logical_and(d[0] == rad, d[1] == azi) for d in targets]
    sources = [(home, jnp.int32(a)) for a in range(n)]
    back = [jnp.logical_and(home == rad, azi == a) for a in range(n)]

    barrier = pltpu.get_barrier_semaphore()
    greeted = jnp.int32(0)
    for device, skip in [*zip(targets, same), *zip(sources, back),
                         (prev, jnp.logical_not(has_prev)), (following, jnp.logical_not(has_next))]:
        @pl.when(jnp.logical_not(skip))
        def _():
            pl.semaphore_signal(barrier, inc=1, device_id=device, device_id_type=MESH)
        greeted = greeted + jnp.where(skip, 0, 1)
    pl.semaphore_wait(barrier, greeted)

    def first_pass(f, act):
        for b in range(n):
            def parts():
                at = pl.ds(azi * width, width)
                if f is None:
                    return kappa.at[pl.ds(b * own, own)], kap.at[:, at], count
                return fields.at[f, pl.ds(b * own, own)], x0.at[f, pl.ds(2, own), at], f

            @pl.when(jnp.logical_not(same[b]))
            def _():
                src, dst, k = parts()
                copy = pltpu.make_async_remote_copy(
                    src, dst, send1.at[k, b], recv1.at[k], device_id=targets[b], device_id_type=MESH)
                copy.start() if act == "start" else copy.wait_send()

            if act == "start":
                @pl.when(same[b])
                def _():
                    src, dst, k = parts()
                    pltpu.make_async_copy(src, dst, recv1.at[k]).start()

    def second_pass(f, act):
        for a in range(n):
            def parts():
                return adv.at[f, :, pl.ds(a * width, width)], out.at[f, pl.ds(spot * own, own)]

            @pl.when(jnp.logical_not(back[a]))
            def _():
                src, dst = parts()
                copy = pltpu.make_async_remote_copy(
                    src, dst, send2.at[f, a], recv2.at[f], device_id=sources[a], device_id_type=MESH)
                copy.start() if act == "start" else copy.wait_send()

            if act == "start":
                @pl.when(back[a])
                def _():
                    src, dst = parts()
                    pltpu.make_async_copy(src, dst, recv2.at[f]).start()

    def halo(x, f, level, act):
        low = pltpu.make_async_remote_copy(
            x.at[f, pl.ds(2, 2)], x.at[f, pl.ds(own + 2, 2)], send_h.at[f, level, 0],
            recv_h.at[f, level, 0], device_id=prev, device_id_type=MESH)
        high = pltpu.make_async_remote_copy(
            x.at[f, pl.ds(own, 2)], x.at[f, pl.ds(0, 2)], send_h.at[f, level, 1],
            recv_h.at[f, level, 1], device_id=following, device_id_type=MESH)

        @pl.when(has_prev)
        def _():
            if act == "start":
                low.start()
            elif act == "send":
                low.wait_send()
            else:
                high.wait_recv()

        @pl.when(has_next)
        def _():
            if act == "start":
                high.start()
            elif act == "send":
                high.wait_send()
            else:
                low.wait_recv()

    lane = lax.broadcasted_iota(jnp.int32, (around, depth), 1)

    def operate(x, f, i):
        u = x[f, i + 2]
        r2m, r1m, r1p, r2p = x[f, i], x[f, i + 1], x[f, i + 3], x[f, i + 4]
        p1p, p1m = pltpu.roll(u, around - 1, 0), pltpu.roll(u, 1, 0)
        p2p, p2m = pltpu.roll(u, around - 2, 0), pltpu.roll(u, 2, 0)
        z1p = jnp.where(lane < depth - 1, pltpu.roll(u, depth - 1, 1), 0.0)
        z1m = jnp.where(lane >= 1, pltpu.roll(u, 1, 1), 0.0)
        z2p = jnp.where(lane < depth - 2, pltpu.roll(u, depth - 2, 1), 0.0)
        z2m = jnp.where(lane >= 2, pltpu.roll(u, 2, 1), 0.0)
        one = (r1p + r1m) + (p1p + p1m) + (z1p + z1m)
        two = (r2p + r2m) + (p2p + p2m) + (z2p + z2m)
        spread = 16.0 * one - two - 90.0 * u
        carried = (srad[f, i] * (8.0 * (r1p - r1m) - (r2p - r2m))
                   + sazi[f, i] * (8.0 * (p1p - p1m) - (p2p - p2m)))
        return u, kap[i] * spread - carried

    def each_row(body):
        def step(i, carry):
            body(i)
            return carry
        lax.fori_loop(0, own, step, 0)

    def clear(f, carry):
        for x in (x0, x1, x2, x3):
            @pl.when(jnp.logical_not(has_prev))
            def _():
                x[f, pl.ds(0, 2)] = jnp.zeros((2, around, depth), jnp.float32)

            @pl.when(jnp.logical_not(has_next))
            def _():
                x[f, pl.ds(own + 2, 2)] = jnp.zeros((2, around, depth), jnp.float32)
        return carry

    first_pass(0, "start")
    first_pass(None, "start")
    for f in range(1, min(AHEAD, count)):
        first_pass(f, "start")
    lax.fori_loop(0, count, clear, 0)
    pltpu.make_async_copy(kap, kap, recv1.at[count]).wait()

    def scale(i):
        kap[i] = kap[i] * (1.0 / 12.0)
    each_row(scale)

    def tick(t, carry):
        def at_stage(lag):
            f = t - lag
            return f, jnp.logical_and(f >= 0, f < count)

        f_next, fine = at_stage(-AHEAD)

        @pl.when(fine)
        def _():
            first_pass(f_next, "start")

        f4, fine4 = at_stage(4)

        @pl.when(fine4)
        def _():
            halo(x3, f4, 3, "recv")

            def body(i):
                u, change = operate(x3, f4, i)
                adv[f4, i] = 0.5 * (x2[f4, i + 2] + u + change)
            each_row(body)
            second_pass(f4, "start")

        f3, fine3 = at_stage(3)

        @pl.when(fine3)
        def _():
            halo(x2, f3, 2, "recv")

            def body(i):
                u, change = operate(x2, f3, i)
                x3[f3, i + 2] = u + change
            each_row(body)
            halo(x3, f3, 3, "start")

        f2, fine2 = at_stage(2)

        @pl.when(fine2)
        def _():
            halo(x1, f2, 1, "recv")

            def body(i):
                u, change = operate(x1, f2, i)
                half = 0.5 * (x0[f2, i + 2] + u + change)
                x2[f2, i + 2] = pltpu.roll(half, shifts[i], 0)
            each_row(body)
            halo(x2, f2, 2, "start")

        f1, fine1 = at_stage(1)

        @pl.when(fine1)
        def _():
            halo(x0, f1, 0, "recv")

            def body(i):
                u, change = operate(x0, f1, i)
                x1[f1, i + 2] = u + change
            each_row(body)
            halo(x1, f1, 1, "start")

        f0, fine0 = at_stage(0)

        @pl.when(fine0)
        def _():
            here = x0.at[f0, pl.ds(2, own)]
            pltpu.make_async_copy(here, here, recv1.at[f0]).wait()
            halo(x0, f0, 0, "start")
        return carry

    lax.fori_loop(0, count + STAGES, tick, 0)

    first_pass(None, "send")

    def finish(f, carry):
        first_pass(f, "send")
        for level, x in enumerate((x0, x1, x2, x3)):
            halo(x, f, level, "send")
        second_pass(f, "send")
        pltpu.make_async_copy(out.at[f], out.at[f], recv2.at[f]).wait()
        return carry
    lax.fori_loop(0, count, finish, 0)


def shards_by_steps(fields, kappa, radial_speed, azimuth_speed, shifts):
    n = lax.axis_size("azi")
    annuli = lax.axis_size("rad")
    count, rows, width, depth = fields.shape
    own, around = rows // n, width * n
    rad, azi = lax.axis_index("rad"), lax.axis_index("azi")
    mine = block_of(rad, azi, n)
    packed = jnp.concatenate(
        [radial_speed * (1.0 / 12.0), azimuth_speed * (1.0 / 12.0),
         jnp.mod(shifts, around).astype(jnp.float32)[None]], axis=0)
    other = lax.ppermute(packed, "rad", [(i, i ^ 1) for i in range(annuli)])
    rightful = jnp.where(mine // n == rad, packed, other)
    rightful = lax.dynamic_slice_in_dim(rightful, (mine % n) * own, own, axis=1)
    srad, sazi = rightful[:count], rightful[count:2 * count]
    turn = rightful[2 * count].astype(jnp.int32)

    tall = pltpu.VMEM((count, own + 4, around, depth), jnp.float32)
    held = 4 * count * around * depth * (4 * (own + 4) + own + own)
    any_space = pl.BlockSpec(memory_space=pl.ANY)
    small = pl.BlockSpec(memory_space=pltpu.SMEM)
    return pl.pallas_call(
        functools.partial(kernel_by_steps, n, n * annuli),
        out_shape=jax.ShapeDtypeStruct(fields.shape, jnp.float32),
        in_specs=[small, small, small, any_space, any_space],
        out_specs=any_space,
        scratch_shapes=[
            tall, tall, tall, tall,
            pltpu.VMEM((count, own, around, depth), jnp.float32),
            pltpu.VMEM((own, around, depth), jnp.float32),
            pltpu.SemaphoreType.DMA((count + 1, n)),
            pltpu.SemaphoreType.DMA((count + 1,)),
            pltpu.SemaphoreType.DMA((count, STAGES, 2)),
            pltpu.SemaphoreType.DMA((count, STAGES, 2)),
            pltpu.SemaphoreType.DMA((count, n)),
            pltpu.SemaphoreType.DMA((count,)),
        ],
        compiler_params=pltpu.CompilerParams(
            collective_id=1, has_side_effects=True, vmem_limit_bytes=held + (8 << 20)),
    )(srad, sazi, turn, fields, kappa)


def solution(mesh):
    placed = (
        P(None, "rad", "azi", None),
        P("rad", "azi", None),
        P(None, "rad"),
        P(None, "rad"),
        P("rad"),
    )
    return jax.shard_map(
        shards, mesh=mesh, in_specs=placed, out_specs=P(None, "rad", "azi", None), check_vma=False
    )
```

```python
import functools

import jax
import jax.numpy as jnp
from jax import lax
from jax.experimental import pallas as pl
from jax.experimental.pallas import tpu as pltpu
from jax.sharding import PartitionSpec as P

MESH = pl.DeviceIdType.MESH
HALO = 8
STAGES = 4
AHEAD = 2
GROUP = 4


def block_of(rad, azi, n):
    column = rad // 2
    odd = lax.rem(column, 2)
    place = azi + odd * (n - 1 - 2 * azi)
    return column * (2 * n) + 2 * place + lax.rem(rad, 2)


def owner_of(block, n):
    column = block // (2 * n)
    t = lax.rem(block, 2 * n)
    odd = lax.rem(column, 2)
    place = t // 2
    return 2 * column + lax.rem(t, 2), place + odd * (n - 1 - 2 * place)


def kernel(n, blocks, srad, sazi, shifts, fields, kappa, out, x0, x1, x2, x3, adv, kap,
           send1, recv1, send_x, recv_x, send_h, recv_h, send2, recv2):
    count, rows, width, depth = fields.shape
    own = rows // n
    around = width * n
    rad, azi = lax.axis_index("rad"), lax.axis_index("azi")
    core = lax.rem(rad, 2)
    mine = block_of(rad, azi, n)
    home = mine // n
    spot = lax.rem(mine, n)
    turn = lax.rem(mine, 2 * n)
    middle = jnp.logical_or(turn == n, turn == n - 1)
    has_prev, has_next = mine > 0, mine < blocks - 1
    from_prev = jnp.logical_and(has_prev, turn != n)
    from_next = jnp.logical_and(has_next, turn != n - 1)
    prev = owner_of(jnp.maximum(mine - 1, 0), n)
    following = owner_of(jnp.minimum(mine + 1, blocks - 1), n)

    def is_me(device):
        return jnp.logical_and(device[0] == rad, device[1] == azi)

    targets = [owner_of(rad * n + b, n) for b in range(n)]
    same = [is_me(d) for d in targets]
    sources = [(home, jnp.int32(a)) for a in range(n)]
    back = [is_me(d) for d in sources]
    across = owner_of(rad * n + n - core * (n + 1), n)
    across_same = is_me(across)
    holders = [(home + 1 - 2 * lax.rem(home, 2), jnp.int32(a)) for a in range(n)]
    not_held = [jnp.logical_or(jnp.logical_not(middle), is_me(d)) for d in holders]

    barrier = pltpu.get_barrier_semaphore()
    greeted = jnp.int32(0)
    for device, skip in [*zip(targets, same), *zip(sources, back), (across, across_same),
                         *zip(holders, not_held), (prev, jnp.logical_not(from_prev)),
                         (following, jnp.logical_not(from_next))]:
        @pl.when(jnp.logical_not(skip))
        def _():
            pl.semaphore_signal(barrier, inc=1, device_id=device, device_id_type=MESH)
        greeted = greeted + jnp.where(skip, 0, 1)
    pl.semaphore_wait(barrier, greeted)

    def move(act, src, dst, send, recv, device, local):
        @pl.when(jnp.logical_not(local))
        def _():
            copy = pltpu.make_async_remote_copy(
                src, dst, send, recv, device_id=device, device_id_type=MESH)
            copy.start() if act == "start" else copy.wait_send()

        if act == "start":
            @pl.when(local)
            def _():
                pltpu.make_async_copy(src, dst, recv).start()

    def held(q):
        return kappa if isinstance(q, int) else fields.at[q - 1]

    def first_pass(q, act):
        at = pl.ds(azi * width, width)
        edge = (1 - core) * (rows - HALO)
        move(act, held(q).at[pl.ds(edge, HALO)], x0.at[q, pl.ds(core * (HALO + own), HALO), at],
             send_x.at[q], recv_x.at[q], across, across_same)
        for b in range(n):
            move(act, held(q).at[pl.ds(b * own, own)], x0.at[q, pl.ds(HALO, own), at],
                 send1.at[q, b], recv1.at[q], targets[b], same[b])

    def second_pass(f, act):
        for a in range(n):
            move(act, adv.at[f, :, pl.ds(a * width, width)], out.at[f, pl.ds(spot * own, own)],
                 send2.at[f, a], recv2.at[f], sources[a], back[a])

    def halo(q, act):
        low = pltpu.make_async_remote_copy(
            x0.at[q, pl.ds(HALO, HALO)], x0.at[q, pl.ds(own + HALO, HALO)], send_h.at[q, 0],
            recv_h.at[q, 0], device_id=prev, device_id_type=MESH)
        high = pltpu.make_async_remote_copy(
            x0.at[q, pl.ds(own, HALO)], x0.at[q, pl.ds(0, HALO)], send_h.at[q, 1],
            recv_h.at[q, 1], device_id=following, device_id_type=MESH)

        @pl.when(from_prev)
        def _():
            if act == "start":
                low.start()
            elif act == "send":
                low.wait_send()
            else:
                high.wait_recv()

        @pl.when(from_next)
        def _():
            if act == "start":
                high.start()
            elif act == "send":
                high.wait_send()
            else:
                low.wait_recv()

        if act == "recv":
            @pl.when(middle)
            def _():
                here = x0.at[q, pl.ds(0, HALO)]
                pltpu.make_async_copy(here, here, recv_x.at[q]).wait()

    lane = lax.broadcasted_iota(jnp.int32, (around, depth), 1)

    def operate(x, f, i, row):
        u = x[i + 2]
        r2m, r1m, r1p, r2p = x[i], x[i + 1], x[i + 3], x[i + 4]
        p1p, p1m = pltpu.roll(u, around - 1, 0), pltpu.roll(u, 1, 0)
        p2p, p2m = pltpu.roll(u, around - 2, 0), pltpu.roll(u, 2, 0)
        z1p = jnp.where(lane < depth - 1, pltpu.roll(u, depth - 1, 1), 0.0)
        z1m = jnp.where(lane >= 1, pltpu.roll(u, 1, 1), 0.0)
        z2p = jnp.where(lane < depth - 2, pltpu.roll(u, depth - 2, 1), 0.0)
        z2m = jnp.where(lane >= 2, pltpu.roll(u, 2, 1), 0.0)
        one = (r1p + r1m) + (p1p + p1m) + (z1p + z1m)
        two = (r2p + r2m) + (p2p + p2m) + (z2p + z2m)
        spread = 16.0 * one - two - 90.0 * u
        carried = (srad[f, row] * (8.0 * (r1p - r1m) - (r2p - r2m))
                   + sazi[f, row] * (8.0 * (p1p - p1m) - (p2p - p2m)))
        return u, kap[row] * spread - carried

    def each_row(length, value, dst):
        group = next(k for k in (GROUP, 2, 1) if length % k == 0)

        def step(i, carry):
            at = [i * group + k for k in range(group)]
            for k, result in [(k, value(k)) for k in at]:
                dst[k] = result
            return carry
        lax.fori_loop(0, length // group, step, 0)

    def clear(q, carry):
        @pl.when(jnp.logical_not(has_prev))
        def _():
            x0[q, pl.ds(0, HALO)] = jnp.zeros((HALO, around, depth), jnp.float32)

        @pl.when(jnp.logical_not(has_next))
        def _():
            x0[q, pl.ds(own + HALO, HALO)] = jnp.zeros((HALO, around, depth), jnp.float32)
        return carry

    def pass_on(q):
        here = x0.at[q, pl.ds(HALO, own)]
        pltpu.make_async_copy(here, here, recv1.at[q]).wait()
        halo(q, "start")

    def begin(q, carry):
        first_pass(q, "start")
        return carry

    first_pass(0, "start")
    lax.fori_loop(1, min(AHEAD, count) + 1, begin, 0)
    lax.fori_loop(0, count + 1, clear, 0)
    pass_on(0)
    halo(0, "recv")

    each_row(own + 2 * HALO, lambda i: x0[0, i] * (1.0 / 12.0), kap)

    def tick(t, carry):
        @pl.when(t + AHEAD <= count)
        def _():
            first_pass(t + AHEAD, "start")

        @pl.when(t <= count)
        def _():
            pass_on(t)

        @pl.when(t >= 2)
        def _():
            q = t - 1
            f = q - 1
            halo(q, "recv")
            base = x0.at[q]

            def value1(i):
                u, change = operate(base, f, i, i + 2)
                return u + change
            each_row(own + 2 * HALO - 4, value1, x1)

            def value2(i):
                u, change = operate(x1, f, i, i + 4)
                half = 0.5 * (base[i + 4] + u + change)
                return pltpu.roll(half, shifts[i + 4], 0)
            each_row(own + 2 * HALO - 8, value2, x2)

            def value3(i):
                u, change = operate(x2, f, i, i + 6)
                return u + change
            each_row(own + 2 * HALO - 12, value3, x3)

            def value4(i):
                u, change = operate(x3, f, i, i + 8)
                return 0.5 * (x2[i + 4] + u + change)
            each_row(own, value4, adv.at[f])
            second_pass(f, "start")
        return carry

    lax.fori_loop(1, count + 2, tick, 0)

    first_pass(0, "send")
    halo(0, "send")

    def finish(f, carry):
        first_pass(f + 1, "send")
        halo(f + 1, "send")
        second_pass(f, "send")
        pltpu.make_async_copy(out.at[f], out.at[f], recv2.at[f]).wait()
        return carry
    lax.fori_loop(0, count, finish, 0)


def shards(fields, kappa, radial_speed, azimuth_speed, shifts):
    n = lax.axis_size("azi")
    annuli = lax.axis_size("rad")
    count, rows, width, depth = fields.shape
    own, around = rows // n, width * n
    if own < HALO or n % 2:
        return shards_by_steps(fields, kappa, radial_speed, azimuth_speed, shifts)
    rad, azi = lax.axis_index("rad"), lax.axis_index("azi")
    mine = block_of(rad, azi, n)
    packed = jnp.concatenate(
        [radial_speed * (1.0 / 12.0), azimuth_speed * (1.0 / 12.0),
         jnp.mod(shifts, around).astype(jnp.float32)[None]], axis=0)
    below = lax.ppermute(packed, "rad", [(i, i + 1) for i in range(annuli - 1)])
    above = lax.ppermute(packed, "rad", [(i + 1, i) for i in range(annuli - 1)])
    wide = jnp.concatenate([below, packed, above], axis=1)
    start = mine * own - HALO - (rad - 1) * rows
    tall = own + 2 * HALO
    wide = lax.dynamic_slice_in_dim(wide, start, tall, axis=1)
    srad, sazi = wide[:count], wide[count:2 * count]
    turn = wide[2 * count].astype(jnp.int32)

    def scratch(*lead):
        return pltpu.VMEM((*lead, around, depth), jnp.float32)

    held = 4 * around * depth * ((count + 2) * tall + 3 * tall + count * own)
    any_space = pl.BlockSpec(memory_space=pl.ANY)
    small = pl.BlockSpec(memory_space=pltpu.SMEM)
    dma = pltpu.SemaphoreType.DMA
    return pl.pallas_call(
        functools.partial(kernel, n, n * annuli),
        out_shape=jax.ShapeDtypeStruct(fields.shape, jnp.float32),
        in_specs=[small, small, small, any_space, any_space],
        out_specs=any_space,
        scratch_shapes=[
            scratch(count + 1, tall), scratch(tall - 4), scratch(tall - 8), scratch(tall - 12),
            scratch(count, own), scratch(tall),
            dma((count + 1, n)), dma((count + 1,)), dma((count + 1,)), dma((count + 1,)),
            dma((count + 1, 2)), dma((count + 1, 2)), dma((count, n)), dma((count,)),
        ],
        compiler_params=pltpu.CompilerParams(
            collective_id=0, has_side_effects=True, vmem_limit_bytes=held + (8 << 20)),
    )(srad, sazi, turn, fields, kappa)


def kernel_by_steps(n, blocks, srad, sazi, shifts, fields, kappa, out, x0, x1, x2, x3, adv, kap,
           send1, recv1, send_h, recv_h, send2, recv2):
    count, rows, width = fields.shape[0], fields.shape[1], fields.shape[2]
    own = rows // n
    around = width * n
    depth = fields.shape[3]
    rad, azi = lax.axis_index("rad"), lax.axis_index("azi")
    mine = block_of(rad, azi, n)
    home = mine // n
    spot = lax.rem(mine, n)
    has_prev, has_next = mine > 0, mine < blocks - 1
    prev = owner_of(jnp.maximum(mine - 1, 0), n)
    following = owner_of(jnp.minimum(mine + 1, blocks - 1), n)
    targets = [owner_of(rad * n + b, n) for b in range(n)]
    same = [jnp.logical_and(d[0] == rad, d[1] == azi) for d in targets]
    sources = [(home, jnp.int32(a)) for a in range(n)]
    back = [jnp.logical_and(home == rad, azi == a) for a in range(n)]

    barrier = pltpu.get_barrier_semaphore()
    greeted = jnp.int32(0)
    for device, skip in [*zip(targets, same), *zip(sources, back),
                         (prev, jnp.logical_not(has_prev)), (following, jnp.logical_not(has_next))]:
        @pl.when(jnp.logical_not(skip))
        def _():
            pl.semaphore_signal(barrier, inc=1, device_id=device, device_id_type=MESH)
        greeted = greeted + jnp.where(skip, 0, 1)
    pl.semaphore_wait(barrier, greeted)

    def first_pass(f, act):
        for b in range(n):
            def parts():
                at = pl.ds(azi * width, width)
                if f is None:
                    return kappa.at[pl.ds(b * own, own)], kap.at[:, at], count
                return fields.at[f, pl.ds(b * own, own)], x0.at[f, pl.ds(2, own), at], f

            @pl.when(jnp.logical_not(same[b]))
            def _():
                src, dst, k = parts()
                copy = pltpu.make_async_remote_copy(
                    src, dst, send1.at[k, b], recv1.at[k], device_id=targets[b], device_id_type=MESH)
                copy.start() if act == "start" else copy.wait_send()

            if act == "start":
                @pl.when(same[b])
                def _():
                    src, dst, k = parts()
                    pltpu.make_async_copy(src, dst, recv1.at[k]).start()

    def second_pass(f, act):
        for a in range(n):
            def parts():
                return adv.at[f, :, pl.ds(a * width, width)], out.at[f, pl.ds(spot * own, own)]

            @pl.when(jnp.logical_not(back[a]))
            def _():
                src, dst = parts()
                copy = pltpu.make_async_remote_copy(
                    src, dst, send2.at[f, a], recv2.at[f], device_id=sources[a], device_id_type=MESH)
                copy.start() if act == "start" else copy.wait_send()

            if act == "start":
                @pl.when(back[a])
                def _():
                    src, dst = parts()
                    pltpu.make_async_copy(src, dst, recv2.at[f]).start()

    def halo(x, f, level, act):
        low = pltpu.make_async_remote_copy(
            x.at[f, pl.ds(2, 2)], x.at[f, pl.ds(own + 2, 2)], send_h.at[f, level, 0],
            recv_h.at[f, level, 0], device_id=prev, device_id_type=MESH)
        high = pltpu.make_async_remote_copy(
            x.at[f, pl.ds(own, 2)], x.at[f, pl.ds(0, 2)], send_h.at[f, level, 1],
            recv_h.at[f, level, 1], device_id=following, device_id_type=MESH)

        @pl.when(has_prev)
        def _():
            if act == "start":
                low.start()
            elif act == "send":
                low.wait_send()
            else:
                high.wait_recv()

        @pl.when(has_next)
        def _():
            if act == "start":
                high.start()
            elif act == "send":
                high.wait_send()
            else:
                low.wait_recv()

    lane = lax.broadcasted_iota(jnp.int32, (around, depth), 1)

    def operate(x, f, i):
        u = x[f, i + 2]
        r2m, r1m, r1p, r2p = x[f, i], x[f, i + 1], x[f, i + 3], x[f, i + 4]
        p1p, p1m = pltpu.roll(u, around - 1, 0), pltpu.roll(u, 1, 0)
        p2p, p2m = pltpu.roll(u, around - 2, 0), pltpu.roll(u, 2, 0)
        z1p = jnp.where(lane < depth - 1, pltpu.roll(u, depth - 1, 1), 0.0)
        z1m = jnp.where(lane >= 1, pltpu.roll(u, 1, 1), 0.0)
        z2p = jnp.where(lane < depth - 2, pltpu.roll(u, depth - 2, 1), 0.0)
        z2m = jnp.where(lane >= 2, pltpu.roll(u, 2, 1), 0.0)
        one = (r1p + r1m) + (p1p + p1m) + (z1p + z1m)
        two = (r2p + r2m) + (p2p + p2m) + (z2p + z2m)
        spread = 16.0 * one - two - 90.0 * u
        carried = (srad[f, i] * (8.0 * (r1p - r1m) - (r2p - r2m))
                   + sazi[f, i] * (8.0 * (p1p - p1m) - (p2p - p2m)))
        return u, kap[i] * spread - carried

    def each_row(body):
        def step(i, carry):
            body(i)
            return carry
        lax.fori_loop(0, own, step, 0)

    def clear(f, carry):
        for x in (x0, x1, x2, x3):
            @pl.when(jnp.logical_not(has_prev))
            def _():
                x[f, pl.ds(0, 2)] = jnp.zeros((2, around, depth), jnp.float32)

            @pl.when(jnp.logical_not(has_next))
            def _():
                x[f, pl.ds(own + 2, 2)] = jnp.zeros((2, around, depth), jnp.float32)
        return carry

    first_pass(0, "start")
    first_pass(None, "start")
    for f in range(1, min(AHEAD, count)):
        first_pass(f, "start")
    lax.fori_loop(0, count, clear, 0)
    pltpu.make_async_copy(kap, kap, recv1.at[count]).wait()

    def scale(i):
        kap[i] = kap[i] * (1.0 / 12.0)
    each_row(scale)

    def tick(t, carry):
        def at_stage(lag):
            f = t - lag
            return f, jnp.logical_and(f >= 0, f < count)

        f_next, fine = at_stage(-AHEAD)

        @pl.when(fine)
        def _():
            first_pass(f_next, "start")

        f4, fine4 = at_stage(4)

        @pl.when(fine4)
        def _():
            halo(x3, f4, 3, "recv")

            def body(i):
                u, change = operate(x3, f4, i)
                adv[f4, i] = 0.5 * (x2[f4, i + 2] + u + change)
            each_row(body)
            second_pass(f4, "start")

        f3, fine3 = at_stage(3)

        @pl.when(fine3)
        def _():
            halo(x2, f3, 2, "recv")

            def body(i):
                u, change = operate(x2, f3, i)
                x3[f3, i + 2] = u + change
            each_row(body)
            halo(x3, f3, 3, "start")

        f2, fine2 = at_stage(2)

        @pl.when(fine2)
        def _():
            halo(x1, f2, 1, "recv")

            def body(i):
                u, change = operate(x1, f2, i)
                half = 0.5 * (x0[f2, i + 2] + u + change)
                x2[f2, i + 2] = pltpu.roll(half, shifts[i], 0)
            each_row(body)
            halo(x2, f2, 2, "start")

        f1, fine1 = at_stage(1)

        @pl.when(fine1)
        def _():
            halo(x0, f1, 0, "recv")

            def body(i):
                u, change = operate(x0, f1, i)
                x1[f1, i + 2] = u + change
            each_row(body)
            halo(x1, f1, 1, "start")

        f0, fine0 = at_stage(0)

        @pl.when(fine0)
        def _():
            here = x0.at[f0, pl.ds(2, own)]
            pltpu.make_async_copy(here, here, recv1.at[f0]).wait()
            halo(x0, f0, 0, "start")
        return carry

    lax.fori_loop(0, count + STAGES, tick, 0)

    first_pass(None, "send")

    def finish(f, carry):
        first_pass(f, "send")
        for level, x in enumerate((x0, x1, x2, x3)):
            halo(x, f, level, "send")
        second_pass(f, "send")
        pltpu.make_async_copy(out.at[f], out.at[f], recv2.at[f]).wait()
        return carry
    lax.fori_loop(0, count, finish, 0)


def shards_by_steps(fields, kappa, radial_speed, azimuth_speed, shifts):
    n = lax.axis_size("azi")
    annuli = lax.axis_size("rad")
    count, rows, width, depth = fields.shape
    own, around = rows // n, width * n
    rad, azi = lax.axis_index("rad"), lax.axis_index("azi")
    mine = block_of(rad, azi, n)
    packed = jnp.concatenate(
        [radial_speed * (1.0 / 12.0), azimuth_speed * (1.0 / 12.0),
         jnp.mod(shifts, around).astype(jnp.float32)[None]], axis=0)
    other = lax.ppermute(packed, "rad", [(i, i ^ 1) for i in range(annuli)])
    rightful = jnp.where(mine // n == rad, packed, other)
    rightful = lax.dynamic_slice_in_dim(rightful, (mine % n) * own, own, axis=1)
    srad, sazi = rightful[:count], rightful[count:2 * count]
    turn = rightful[2 * count].astype(jnp.int32)

    tall = pltpu.VMEM((count, own + 4, around, depth), jnp.float32)
    held = 4 * count * around * depth * (4 * (own + 4) + own + own)
    any_space = pl.BlockSpec(memory_space=pl.ANY)
    small = pl.BlockSpec(memory_space=pltpu.SMEM)
    return pl.pallas_call(
        functools.partial(kernel_by_steps, n, n * annuli),
        out_shape=jax.ShapeDtypeStruct(fields.shape, jnp.float32),
        in_specs=[small, small, small, any_space, any_space],
        out_specs=any_space,
        scratch_shapes=[
            tall, tall, tall, tall,
            pltpu.VMEM((count, own, around, depth), jnp.float32),
            pltpu.VMEM((own, around, depth), jnp.float32),
            pltpu.SemaphoreType.DMA((count + 1, n)),
            pltpu.SemaphoreType.DMA((count + 1,)),
            pltpu.SemaphoreType.DMA((count, STAGES, 2)),
            pltpu.SemaphoreType.DMA((count, STAGES, 2)),
            pltpu.SemaphoreType.DMA((count, n)),
            pltpu.SemaphoreType.DMA((count,)),
        ],
        compiler_params=pltpu.CompilerParams(
            collective_id=1, has_side_effects=True, vmem_limit_bytes=held + (8 << 20)),
    )(srad, sazi, turn, fields, kappa)


def solution(mesh):
    placed = (
        P(None, "rad", "azi", None),
        P("rad", "azi", None),
        P(None, "rad"),
        P(None, "rad"),
        P("rad"),
    )
    return jax.shard_map(
        shards, mesh=mesh, in_specs=placed, out_specs=P(None, "rad", "azi", None), check_vma=False
    )
```

```python
import functools

import jax
import jax.numpy as jnp
from jax import lax
from jax.experimental import pallas as pl
from jax.experimental.pallas import tpu as pltpu
from jax.sharding import PartitionSpec as P

MESH = pl.DeviceIdType.MESH
HALO = 8
STAGES = 4
AHEAD = 2
GROUP = 4


def block_of(rad, azi, n):
    column = rad // 2
    odd = lax.rem(column, 2)
    place = azi + odd * (n - 1 - 2 * azi)
    return column * (2 * n) + 2 * place + lax.rem(rad, 2)


def owner_of(block, n):
    column = block // (2 * n)
    t = lax.rem(block, 2 * n)
    odd = lax.rem(column, 2)
    place = t // 2
    return 2 * column + lax.rem(t, 2), place + odd * (n - 1 - 2 * place)


def kernel(n, blocks, fast_r, fast_p, shifts, fields, kappa, out, x0, x1, x2, x3, adv, kap,
           near_r, near_p, near_s, srad, sazi, turns, send_n, recv_n, load_n, send1, recv1, send_x, recv_x, send_h, recv_h, send2, recv2):
    count, rows, width, depth = fields.shape
    own = rows // n
    around = width * n
    rad, azi = lax.axis_index("rad"), lax.axis_index("azi")
    core = lax.rem(rad, 2)
    mine = block_of(rad, azi, n)
    home = mine // n
    spot = lax.rem(mine, n)
    turn = lax.rem(mine, 2 * n)
    middle = jnp.logical_or(turn == n, turn == n - 1)
    has_prev, has_next = mine > 0, mine < blocks - 1
    from_prev = jnp.logical_and(has_prev, turn != n)
    from_next = jnp.logical_and(has_next, turn != n - 1)
    prev = owner_of(jnp.maximum(mine - 1, 0), n)
    following = owner_of(jnp.minimum(mine + 1, blocks - 1), n)

    def is_me(device):
        return jnp.logical_and(device[0] == rad, device[1] == azi)

    targets = [owner_of(rad * n + b, n) for b in range(n)]
    same = [is_me(d) for d in targets]
    sources = [(home, jnp.int32(a)) for a in range(n)]
    back = [is_me(d) for d in sources]
    across = owner_of(rad * n + n - core * (n + 1), n)
    across_same = is_me(across)
    holders = [(home + 1 - 2 * lax.rem(home, 2), jnp.int32(a)) for a in range(n)]
    not_held = [jnp.logical_or(jnp.logical_not(middle), is_me(d)) for d in holders]

    below_in, above_in = rad > 0, rad < blocks // n - 1
    below = (jnp.maximum(rad - 1, 0), azi)
    above = (jnp.minimum(rad + 1, blocks // n - 1), azi)

    barrier = pltpu.get_barrier_semaphore()
    greeted = jnp.int32(0)
    for device, skip in [*zip(targets, same), *zip(sources, back), (across, across_same),
                         *zip(holders, not_held), (prev, jnp.logical_not(from_prev)),
                         (below, jnp.logical_not(below_in)), (above, jnp.logical_not(above_in)),
                         (following, jnp.logical_not(from_next))]:
        @pl.when(jnp.logical_not(skip))
        def _():
            pl.semaphore_signal(barrier, inc=1, device_id=device, device_id_type=MESH)
        greeted = greeted + jnp.where(skip, 0, 1)
    pl.semaphore_wait(barrier, greeted)

    def move(act, src, dst, send, recv, device, local):
        @pl.when(jnp.logical_not(local))
        def _():
            copy = pltpu.make_async_remote_copy(
                src, dst, send, recv, device_id=device, device_id_type=MESH)
            copy.start() if act == "start" else copy.wait_send()

        if act == "start":
            @pl.when(local)
            def _():
                pltpu.make_async_copy(src, dst, recv).start()

    def held(q):
        return kappa if isinstance(q, int) else fields.at[q - 1]

    def first_pass(q, act):
        at = pl.ds(azi * width, width)
        edge = (1 - core) * (rows - HALO)
        move(act, held(q).at[pl.ds(edge, HALO)], x0.at[q, pl.ds(core * (HALO + own), HALO), at],
             send_x.at[q], recv_x.at[q], across, across_same)
        for b in range(n):
            move(act, held(q).at[pl.ds(b * own, own)], x0.at[q, pl.ds(HALO, own), at],
                 send1.at[q, b], recv1.at[q], targets[b], same[b])

    def second_pass(f, act):
        for a in range(n):
            move(act, adv.at[f, :, pl.ds(a * width, width)], out.at[f, pl.ds(spot * own, own)],
                 send2.at[f, a], recv2.at[f], sources[a], back[a])

    def halo(q, act):
        low = pltpu.make_async_remote_copy(
            x0.at[q, pl.ds(HALO, HALO)], x0.at[q, pl.ds(own + HALO, HALO)], send_h.at[q, 0],
            recv_h.at[q, 0], device_id=prev, device_id_type=MESH)
        high = pltpu.make_async_remote_copy(
            x0.at[q, pl.ds(own, HALO)], x0.at[q, pl.ds(0, HALO)], send_h.at[q, 1],
            recv_h.at[q, 1], device_id=following, device_id_type=MESH)

        @pl.when(from_prev)
        def _():
            if act == "start":
                low.start()
            elif act == "send":
                low.wait_send()
            else:
                high.wait_recv()

        @pl.when(from_next)
        def _():
            if act == "start":
                high.start()
            elif act == "send":
                high.wait_send()
            else:
                low.wait_recv()

        if act == "recv":
            @pl.when(middle)
            def _():
                here = x0.at[q, pl.ds(0, HALO)]
                pltpu.make_async_copy(here, here, recv_x.at[q]).wait()

    small = ((fast_r, near_r, srad), (fast_p, near_p, sazi), (shifts, near_s, turns))

    def speeds(act):
        for k, (mine_k, near, held_k) in enumerate(small):
            for side, device, there in ((0, below, below_in), (1, above, above_in)):
                slot = 1 - side
                copy = pltpu.make_async_remote_copy(
                    mine_k, near.at[slot], send_n.at[k, side], recv_n.at[k, slot],
                    device_id=device, device_id_type=MESH)
                arrived = pltpu.make_async_remote_copy(
                    mine_k, near.at[side], send_n.at[k, slot], recv_n.at[k, side],
                    device_id=device, device_id_type=MESH)
                inward = pltpu.make_async_copy(
                    near.at[side], held_k.at[2 * side], load_n.at[k, side])

                @pl.when(there)
                def _():
                    if act == "start":
                        copy.start()
                    elif act == "send":
                        copy.wait_send()
                    elif act == "recv":
                        arrived.wait_recv()
                        inward.start()
                    else:
                        inward.wait()
            own_copy = pltpu.make_async_copy(mine_k, held_k.at[1], load_n.at[k, 2])
            if act == "start":
                own_copy.start()
            elif act == "load":
                own_copy.wait()

    first_row = mine * own - HALO
    total_rows = blocks * own

    def of_row(table, row, *lead):
        at = first_row + row
        inside = jnp.logical_and(at >= 0, at < total_rows)
        at = jnp.clip(at, 0, total_rows - 1) - (rad - 1) * rows
        return jnp.where(inside, table[(at // rows, *lead, lax.rem(at, rows))], 0)

    lane = lax.broadcasted_iota(jnp.int32, (around, depth), 1)

    def operate(x, f, i, row):
        u = x[i + 2]
        r2m, r1m, r1p, r2p = x[i], x[i + 1], x[i + 3], x[i + 4]
        p1p, p1m = pltpu.roll(u, around - 1, 0), pltpu.roll(u, 1, 0)
        p2p, p2m = pltpu.roll(u, around - 2, 0), pltpu.roll(u, 2, 0)
        z1p = jnp.where(lane < depth - 1, pltpu.roll(u, depth - 1, 1), 0.0)
        z1m = jnp.where(lane >= 1, pltpu.roll(u, 1, 1), 0.0)
        z2p = jnp.where(lane < depth - 2, pltpu.roll(u, depth - 2, 1), 0.0)
        z2m = jnp.where(lane >= 2, pltpu.roll(u, 2, 1), 0.0)
        one = (r1p + r1m) + (p1p + p1m) + (z1p + z1m)
        two = (r2p + r2m) + (p2p + p2m) + (z2p + z2m)
        spread = 16.0 * one - two - 90.0 * u
        fast = of_row(srad, row, f) * (1.0 / 12.0)
        slow = of_row(sazi, row, f) * (1.0 / 12.0)
        carried = (fast * (8.0 * (r1p - r1m) - (r2p - r2m))
                   + slow * (8.0 * (p1p - p1m) - (p2p - p2m)))
        return u, kap[row] * spread - carried

    def each_row(length, value, dst):
        group = next(k for k in (GROUP, 2, 1) if length % k == 0)

        def step(i, carry):
            at = [i * group + k for k in range(group)]
            for k, result in [(k, value(k)) for k in at]:
                dst[k] = result
            return carry
        lax.fori_loop(0, length // group, step, 0)

    def clear(q, carry):
        @pl.when(jnp.logical_not(has_prev))
        def _():
            x0[q, pl.ds(0, HALO)] = jnp.zeros((HALO, around, depth), jnp.float32)

        @pl.when(jnp.logical_not(has_next))
        def _():
            x0[q, pl.ds(own + HALO, HALO)] = jnp.zeros((HALO, around, depth), jnp.float32)
        return carry

    def pass_on(q):
        here = x0.at[q, pl.ds(HALO, own)]
        pltpu.make_async_copy(here, here, recv1.at[q]).wait()
        halo(q, "start")

    def begin(q, carry):
        first_pass(q, "start")
        return carry

    first_pass(0, "start")
    speeds("start")
    lax.fori_loop(1, min(AHEAD, count) + 1, begin, 0)
    lax.fori_loop(0, count + 1, clear, 0)
    speeds("recv")
    pass_on(0)
    pass_on(1)
    speeds("load")
    halo(0, "recv")

    each_row(own + 2 * HALO, lambda i: x0[0, i] * (1.0 / 12.0), kap)

    def tick(t, carry):
        @pl.when(t + AHEAD <= count)
        def _():
            first_pass(t + AHEAD, "start")

        q = t
        f = q - 1
        halo(q, "recv")
        base = x0.at[q]

        def value1(i):
            u, change = operate(base, f, i, i + 2)
            return u + change
        each_row(own + 2 * HALO - 4, value1, x1)

        def value2(i):
            u, change = operate(x1, f, i, i + 4)
            half = 0.5 * (base[i + 4] + u + change)
            return pltpu.roll(half, of_row(turns, i + 4, 0), 0)
        each_row(own + 2 * HALO - 8, value2, x2)

        @pl.when(t < count)
        def _():
            pass_on(t + 1)

        def value3(i):
            u, change = operate(x2, f, i, i + 6)
            return u + change
        each_row(own + 2 * HALO - 12, value3, x3)

        def value4(i):
            u, change = operate(x3, f, i, i + 8)
            return 0.5 * (x2[i + 4] + u + change)
        each_row(own, value4, adv.at[f])
        second_pass(f, "start")
        return carry

    lax.fori_loop(1, count + 1, tick, 0)

    speeds("send")
    first_pass(0, "send")
    halo(0, "send")

    def finish(f, carry):
        first_pass(f + 1, "send")
        halo(f + 1, "send")
        second_pass(f, "send")
        pltpu.make_async_copy(out.at[f], out.at[f], recv2.at[f]).wait()
        return carry
    lax.fori_loop(0, count, finish, 0)


def shards(fields, kappa, radial_speed, azimuth_speed, shifts):
    n = lax.axis_size("azi")
    annuli = lax.axis_size("rad")
    count, rows, width, depth = fields.shape
    own, around = rows // n, width * n
    if own < HALO or n % 2:
        return shards_by_steps(fields, kappa, radial_speed, azimuth_speed, shifts)
    tall = own + 2 * HALO

    def scratch(*lead):
        return pltpu.VMEM((*lead, around, depth), jnp.float32)

    held = 4 * around * depth * ((count + 2) * tall + 3 * tall + count * own)
    any_space = pl.BlockSpec(memory_space=pl.ANY)
    table = radial_speed.shape
    dma = pltpu.SemaphoreType.DMA
    return pl.pallas_call(
        functools.partial(kernel, n, n * annuli),
        out_shape=jax.ShapeDtypeStruct(fields.shape, jnp.float32),
        in_specs=[any_space] * 5,
        out_specs=any_space,
        scratch_shapes=[
            scratch(count + 1, tall), scratch(tall - 4), scratch(tall - 8), scratch(tall - 12),
            scratch(count, own), scratch(tall),
            pltpu.VMEM((2, *table), jnp.float32), pltpu.VMEM((2, *table), jnp.float32),
            pltpu.VMEM((2, 1, rows), jnp.int32), pltpu.SMEM((3, *table), jnp.float32),
            pltpu.SMEM((3, *table), jnp.float32), pltpu.SMEM((3, 1, rows), jnp.int32),
            dma((3, 2)), dma((3, 2)), dma((3, 3)),
            dma((count + 1, n)), dma((count + 1,)), dma((count + 1,)), dma((count + 1,)),
            dma((count + 1, 2)), dma((count + 1, 2)), dma((count, n)), dma((count,)),
        ],
        compiler_params=pltpu.CompilerParams(
            collective_id=0, has_side_effects=True, vmem_limit_bytes=held + (8 << 20)),
    )(radial_speed, azimuth_speed, shifts[None], fields, kappa)


def kernel_by_steps(n, blocks, srad, sazi, shifts, fields, kappa, out, x0, x1, x2, x3, adv, kap,
           send1, recv1, send_h, recv_h, send2, recv2):
    count, rows, width = fields.shape[0], fields.shape[1], fields.shape[2]
    own = rows // n
    around = width * n
    depth = fields.shape[3]
    rad, azi = lax.axis_index("rad"), lax.axis_index("azi")
    mine = block_of(rad, azi, n)
    home = mine // n
    spot = lax.rem(mine, n)
    has_prev, has_next = mine > 0, mine < blocks - 1
    prev = owner_of(jnp.maximum(mine - 1, 0), n)
    following = owner_of(jnp.minimum(mine + 1, blocks - 1), n)
    targets = [owner_of(rad * n + b, n) for b in range(n)]
    same = [jnp.logical_and(d[0] == rad, d[1] == azi) for d in targets]
    sources = [(home, jnp.int32(a)) for a in range(n)]
    back = [jnp.logical_and(home == rad, azi == a) for a in range(n)]

    barrier = pltpu.get_barrier_semaphore()
    greeted = jnp.int32(0)
    for device, skip in [*zip(targets, same), *zip(sources, back),
                         (prev, jnp.logical_not(has_prev)), (following, jnp.logical_not(has_next))]:
        @pl.when(jnp.logical_not(skip))
        def _():
            pl.semaphore_signal(barrier, inc=1, device_id=device, device_id_type=MESH)
        greeted = greeted + jnp.where(skip, 0, 1)
    pl.semaphore_wait(barrier, greeted)

    def first_pass(f, act):
        for b in range(n):
            def parts():
                at = pl.ds(azi * width, width)
                if f is None:
                    return kappa.at[pl.ds(b * own, own)], kap.at[:, at], count
                return fields.at[f, pl.ds(b * own, own)], x0.at[f, pl.ds(2, own), at], f

            @pl.when(jnp.logical_not(same[b]))
            def _():
                src, dst, k = parts()
                copy = pltpu.make_async_remote_copy(
                    src, dst, send1.at[k, b], recv1.at[k], device_id=targets[b], device_id_type=MESH)
                copy.start() if act == "start" else copy.wait_send()

            if act == "start":
                @pl.when(same[b])
                def _():
                    src, dst, k = parts()
                    pltpu.make_async_copy(src, dst, recv1.at[k]).start()

    def second_pass(f, act):
        for a in range(n):
            def parts():
                return adv.at[f, :, pl.ds(a * width, width)], out.at[f, pl.ds(spot * own, own)]

            @pl.when(jnp.logical_not(back[a]))
            def _():
                src, dst = parts()
                copy = pltpu.make_async_remote_copy(
                    src, dst, send2.at[f, a], recv2.at[f], device_id=sources[a], device_id_type=MESH)
                copy.start() if act == "start" else copy.wait_send()

            if act == "start":
                @pl.when(back[a])
                def _():
                    src, dst = parts()
                    pltpu.make_async_copy(src, dst, recv2.at[f]).start()

    def halo(x, f, level, act):
        low = pltpu.make_async_remote_copy(
            x.at[f, pl.ds(2, 2)], x.at[f, pl.ds(own + 2, 2)], send_h.at[f, level, 0],
            recv_h.at[f, level, 0], device_id=prev, device_id_type=MESH)
        high = pltpu.make_async_remote_copy(
            x.at[f, pl.ds(own, 2)], x.at[f, pl.ds(0, 2)], send_h.at[f, level, 1],
            recv_h.at[f, level, 1], device_id=following, device_id_type=MESH)

        @pl.when(has_prev)
        def _():
            if act == "start":
                low.start()
            elif act == "send":
                low.wait_send()
            else:
                high.wait_recv()

        @pl.when(has_next)
        def _():
            if act == "start":
                high.start()
            elif act == "send":
                high.wait_send()
            else:
                low.wait_recv()

    lane = lax.broadcasted_iota(jnp.int32, (around, depth), 1)

    def operate(x, f, i):
        u = x[f, i + 2]
        r2m, r1m, r1p, r2p = x[f, i], x[f, i + 1], x[f, i + 3], x[f, i + 4]
        p1p, p1m = pltpu.roll(u, around - 1, 0), pltpu.roll(u, 1, 0)
        p2p, p2m = pltpu.roll(u, around - 2, 0), pltpu.roll(u, 2, 0)
        z1p = jnp.where(lane < depth - 1, pltpu.roll(u, depth - 1, 1), 0.0)
        z1m = jnp.where(lane >= 1, pltpu.roll(u, 1, 1), 0.0)
        z2p = jnp.where(lane < depth - 2, pltpu.roll(u, depth - 2, 1), 0.0)
        z2m = jnp.where(lane >= 2, pltpu.roll(u, 2, 1), 0.0)
        one = (r1p + r1m) + (p1p + p1m) + (z1p + z1m)
        two = (r2p + r2m) + (p2p + p2m) + (z2p + z2m)
        spread = 16.0 * one - two - 90.0 * u
        carried = (srad[f, i] * (8.0 * (r1p - r1m) - (r2p - r2m))
                   + sazi[f, i] * (8.0 * (p1p - p1m) - (p2p - p2m)))
        return u, kap[i] * spread - carried

    def each_row(body):
        def step(i, carry):
            body(i)
            return carry
        lax.fori_loop(0, own, step, 0)

    def clear(f, carry):
        for x in (x0, x1, x2, x3):
            @pl.when(jnp.logical_not(has_prev))
            def _():
                x[f, pl.ds(0, 2)] = jnp.zeros((2, around, depth), jnp.float32)

            @pl.when(jnp.logical_not(has_next))
            def _():
                x[f, pl.ds(own + 2, 2)] = jnp.zeros((2, around, depth), jnp.float32)
        return carry

    first_pass(0, "start")
    first_pass(None, "start")
    for f in range(1, min(AHEAD, count)):
        first_pass(f, "start")
    lax.fori_loop(0, count, clear, 0)
    pltpu.make_async_copy(kap, kap, recv1.at[count]).wait()

    def scale(i):
        kap[i] = kap[i] * (1.0 / 12.0)
    each_row(scale)

    def tick(t, carry):
        def at_stage(lag):
            f = t - lag
            return f, jnp.logical_and(f >= 0, f < count)

        f_next, fine = at_stage(-AHEAD)

        @pl.when(fine)
        def _():
            first_pass(f_next, "start")

        f4, fine4 = at_stage(4)

        @pl.when(fine4)
        def _():
            halo(x3, f4, 3, "recv")

            def body(i):
                u, change = operate(x3, f4, i)
                adv[f4, i] = 0.5 * (x2[f4, i + 2] + u + change)
            each_row(body)
            second_pass(f4, "start")

        f3, fine3 = at_stage(3)

        @pl.when(fine3)
        def _():
            halo(x2, f3, 2, "recv")

            def body(i):
                u, change = operate(x2, f3, i)
                x3[f3, i + 2] = u + change
            each_row(body)
            halo(x3, f3, 3, "start")

        f2, fine2 = at_stage(2)

        @pl.when(fine2)
        def _():
            halo(x1, f2, 1, "recv")

            def body(i):
                u, change = operate(x1, f2, i)
                half = 0.5 * (x0[f2, i + 2] + u + change)
                x2[f2, i + 2] = pltpu.roll(half, shifts[i], 0)
            each_row(body)
            halo(x2, f2, 2, "start")

        f1, fine1 = at_stage(1)

        @pl.when(fine1)
        def _():
            halo(x0, f1, 0, "recv")

            def body(i):
                u, change = operate(x0, f1, i)
                x1[f1, i + 2] = u + change
            each_row(body)
            halo(x1, f1, 1, "start")

        f0, fine0 = at_stage(0)

        @pl.when(fine0)
        def _():
            here = x0.at[f0, pl.ds(2, own)]
            pltpu.make_async_copy(here, here, recv1.at[f0]).wait()
            halo(x0, f0, 0, "start")
        return carry

    lax.fori_loop(0, count + STAGES, tick, 0)

    first_pass(None, "send")

    def finish(f, carry):
        first_pass(f, "send")
        for level, x in enumerate((x0, x1, x2, x3)):
            halo(x, f, level, "send")
        second_pass(f, "send")
        pltpu.make_async_copy(out.at[f], out.at[f], recv2.at[f]).wait()
        return carry
    lax.fori_loop(0, count, finish, 0)


def shards_by_steps(fields, kappa, radial_speed, azimuth_speed, shifts):
    n = lax.axis_size("azi")
    annuli = lax.axis_size("rad")
    count, rows, width, depth = fields.shape
    own, around = rows // n, width * n
    rad, azi = lax.axis_index("rad"), lax.axis_index("azi")
    mine = block_of(rad, azi, n)
    packed = jnp.concatenate(
        [radial_speed * (1.0 / 12.0), azimuth_speed * (1.0 / 12.0),
         jnp.mod(shifts, around).astype(jnp.float32)[None]], axis=0)
    other = lax.ppermute(packed, "rad", [(i, i ^ 1) for i in range(annuli)])
    rightful = jnp.where(mine // n == rad, packed, other)
    rightful = lax.dynamic_slice_in_dim(rightful, (mine % n) * own, own, axis=1)
    srad, sazi = rightful[:count], rightful[count:2 * count]
    turn = rightful[2 * count].astype(jnp.int32)

    tall = pltpu.VMEM((count, own + 4, around, depth), jnp.float32)
    held = 4 * count * around * depth * (4 * (own + 4) + own + own)
    any_space = pl.BlockSpec(memory_space=pl.ANY)
    small = pl.BlockSpec(memory_space=pltpu.SMEM)
    return pl.pallas_call(
        functools.partial(kernel_by_steps, n, n * annuli),
        out_shape=jax.ShapeDtypeStruct(fields.shape, jnp.float32),
        in_specs=[small, small, small, any_space, any_space],
        out_specs=any_space,
        scratch_shapes=[
            tall, tall, tall, tall,
            pltpu.VMEM((count, own, around, depth), jnp.float32),
            pltpu.VMEM((own, around, depth), jnp.float32),
            pltpu.SemaphoreType.DMA((count + 1, n)),
            pltpu.SemaphoreType.DMA((count + 1,)),
            pltpu.SemaphoreType.DMA((count, STAGES, 2)),
            pltpu.SemaphoreType.DMA((count, STAGES, 2)),
            pltpu.SemaphoreType.DMA((count, n)),
            pltpu.SemaphoreType.DMA((count,)),
        ],
        compiler_params=pltpu.CompilerParams(
            collective_id=1, has_side_effects=True, vmem_limit_bytes=held + (8 << 20)),
    )(srad, sazi, turn, fields, kappa)


def solution(mesh):
    placed = (
        P(None, "rad", "azi", None),
        P("rad", "azi", None),
        P(None, "rad"),
        P(None, "rad"),
        P("rad"),
    )
    return jax.shard_map(
        shards, mesh=mesh, in_specs=placed, out_specs=P(None, "rad", "azi", None), check_vma=False
    )
```

```python
import functools

import jax
import jax.numpy as jnp
from jax import lax
from jax.experimental import pallas as pl
from jax.experimental.pallas import tpu as pltpu
from jax.sharding import PartitionSpec as P

MESH = pl.DeviceIdType.MESH
HALO = 8
STAGES = 4
AHEAD = 2
GROUP = 4


def block_of(rad, azi, n):
    column = rad // 2
    odd = lax.rem(column, 2)
    place = azi + odd * (n - 1 - 2 * azi)
    return column * (2 * n) + 2 * place + lax.rem(rad, 2)


def owner_of(block, n):
    column = block // (2 * n)
    t = lax.rem(block, 2 * n)
    odd = lax.rem(column, 2)
    place = t // 2
    return 2 * column + lax.rem(t, 2), place + odd * (n - 1 - 2 * place)


def kernel(n, blocks, fast_r, fast_p, shifts, fields, kappa, out, x0, x1, x2, x3, adv, kap,
           near_r, near_p, near_s, srad, sazi, turns, send_n, recv_n, load_n, send1, recv1, send_x, recv_x, send_h, recv_h, send2, recv2):
    count, rows, width, depth = fields.shape
    own = rows // n
    around = width * n
    rad, azi = lax.axis_index("rad"), lax.axis_index("azi")
    core = lax.rem(rad, 2)
    mine = block_of(rad, azi, n)
    home = mine // n
    spot = lax.rem(mine, n)
    turn = lax.rem(mine, 2 * n)
    middle = jnp.logical_or(turn == n, turn == n - 1)
    has_prev, has_next = mine > 0, mine < blocks - 1
    from_prev = jnp.logical_and(has_prev, turn != n)
    from_next = jnp.logical_and(has_next, turn != n - 1)
    prev = owner_of(jnp.maximum(mine - 1, 0), n)
    following = owner_of(jnp.minimum(mine + 1, blocks - 1), n)

    def is_me(device):
        return jnp.logical_and(device[0] == rad, device[1] == azi)

    targets = [owner_of(rad * n + b, n) for b in range(n)]
    same = [is_me(d) for d in targets]
    sources = [(home, jnp.int32(a)) for a in range(n)]
    back = [is_me(d) for d in sources]
    across = owner_of(rad * n + n - core * (n + 1), n)
    across_same = is_me(across)
    holders = [(home + 1 - 2 * lax.rem(home, 2), jnp.int32(a)) for a in range(n)]
    not_held = [jnp.logical_or(jnp.logical_not(middle), is_me(d)) for d in holders]

    below_in, above_in = rad > 0, rad < blocks // n - 1
    below = (jnp.maximum(rad - 1, 0), azi)
    above = (jnp.minimum(rad + 1, blocks // n - 1), azi)

    barrier = pltpu.get_barrier_semaphore()
    greeted = jnp.int32(0)
    for device, skip in [*zip(targets, same), *zip(sources, back), (across, across_same),
                         *zip(holders, not_held), (prev, jnp.logical_not(from_prev)),
                         (below, jnp.logical_not(below_in)), (above, jnp.logical_not(above_in)),
                         (following, jnp.logical_not(from_next))]:
        @pl.when(jnp.logical_not(skip))
        def _():
            pl.semaphore_signal(barrier, inc=1, device_id=device, device_id_type=MESH)
        greeted = greeted + jnp.where(skip, 0, 1)
    pl.semaphore_wait(barrier, greeted)

    def move(act, src, dst, send, recv, device, local):
        @pl.when(jnp.logical_not(local))
        def _():
            copy = pltpu.make_async_remote_copy(
                src, dst, send, recv, device_id=device, device_id_type=MESH)
            copy.start() if act == "start" else copy.wait_send()

        if act == "start":
            @pl.when(local)
            def _():
                pltpu.make_async_copy(src, dst, recv).start()

    def held(q):
        return kappa if isinstance(q, int) else fields.at[q - 1]

    def first_pass(q, act):
        at = pl.ds(azi * width, width)
        edge = (1 - core) * (rows - HALO)
        move(act, held(q).at[pl.ds(edge, HALO)], x0.at[q, pl.ds(core * (HALO + own), HALO), at],
             send_x.at[q], recv_x.at[q], across, across_same)
        for b in range(n):
            move(act, held(q).at[pl.ds(b * own, own)], x0.at[q, pl.ds(HALO, own), at],
                 send1.at[q, b], recv1.at[q], targets[b], same[b])

    def second_pass(f, act):
        for a in range(n):
            move(act, adv.at[f, :, pl.ds(a * width, width)], out.at[f, pl.ds(spot * own, own)],
                 send2.at[f, a], recv2.at[f], sources[a], back[a])

    def halo(q, act):
        low = pltpu.make_async_remote_copy(
            x0.at[q, pl.ds(HALO, HALO)], x0.at[q, pl.ds(own + HALO, HALO)], send_h.at[q, 0],
            recv_h.at[q, 0], device_id=prev, device_id_type=MESH)
        high = pltpu.make_async_remote_copy(
            x0.at[q, pl.ds(own, HALO)], x0.at[q, pl.ds(0, HALO)], send_h.at[q, 1],
            recv_h.at[q, 1], device_id=following, device_id_type=MESH)

        @pl.when(from_prev)
        def _():
            if act == "start":
                low.start()
            elif act == "send":
                low.wait_send()
            else:
                high.wait_recv()

        @pl.when(from_next)
        def _():
            if act == "start":
                high.start()
            elif act == "send":
                high.wait_send()
            else:
                low.wait_recv()

        if act == "recv":
            @pl.when(middle)
            def _():
                here = x0.at[q, pl.ds(0, HALO)]
                pltpu.make_async_copy(here, here, recv_x.at[q]).wait()

    small = ((fast_r, near_r, srad), (fast_p, near_p, sazi), (shifts, near_s, turns))

    def speeds(act):
        for k, (mine_k, near, held_k) in enumerate(small):
            for side, device, there in ((0, below, below_in), (1, above, above_in)):
                slot = 1 - side
                copy = pltpu.make_async_remote_copy(
                    mine_k, near.at[slot], send_n.at[k, side], recv_n.at[k, slot],
                    device_id=device, device_id_type=MESH)
                arrived = pltpu.make_async_remote_copy(
                    mine_k, near.at[side], send_n.at[k, slot], recv_n.at[k, side],
                    device_id=device, device_id_type=MESH)
                inward = pltpu.make_async_copy(
                    near.at[side], held_k.at[2 * side], load_n.at[k, side])

                @pl.when(there)
                def _():
                    if act == "start":
                        copy.start()
                    elif act == "send":
                        copy.wait_send()
                    elif act == "recv":
                        arrived.wait_recv()
                        inward.start()
                    else:
                        inward.wait()
            own_copy = pltpu.make_async_copy(mine_k, held_k.at[1], load_n.at[k, 2])
            if act == "start":
                own_copy.start()
            elif act == "load":
                own_copy.wait()

    first_row = mine * own - HALO
    total_rows = blocks * own

    def of_row(table, row, *lead):
        at = first_row + row
        inside = jnp.logical_and(at >= 0, at < total_rows)
        at = jnp.clip(at, 0, total_rows - 1) - (rad - 1) * rows
        return jnp.where(inside, table[(at // rows, *lead, lax.rem(at, rows))], 0)

    lane = lax.broadcasted_iota(jnp.int32, (around, depth), 1)

    def operate(x, f, i, row):
        u = x[i + 2]
        r2m, r1m, r1p, r2p = x[i], x[i + 1], x[i + 3], x[i + 4]
        p1p, p1m = pltpu.roll(u, around - 1, 0), pltpu.roll(u, 1, 0)
        p2p, p2m = pltpu.roll(u, around - 2, 0), pltpu.roll(u, 2, 0)
        z1p = jnp.where(lane < depth - 1, pltpu.roll(u, depth - 1, 1), 0.0)
        z1m = jnp.where(lane >= 1, pltpu.roll(u, 1, 1), 0.0)
        z2p = jnp.where(lane < depth - 2, pltpu.roll(u, depth - 2, 1), 0.0)
        z2m = jnp.where(lane >= 2, pltpu.roll(u, 2, 1), 0.0)
        one = (r1p + r1m) + (p1p + p1m) + (z1p + z1m)
        two = (r2p + r2m) + (p2p + p2m) + (z2p + z2m)
        spread = 16.0 * one - two - 90.0 * u
        fast = of_row(srad, row, f) * (1.0 / 12.0)
        slow = of_row(sazi, row, f) * (1.0 / 12.0)
        carried = (fast * (8.0 * (r1p - r1m) - (r2p - r2m))
                   + slow * (8.0 * (p1p - p1m) - (p2p - p2m)))
        return u, kap[row] * spread - carried

    def each_row(length, value, dst):
        group = next(k for k in (GROUP, 2, 1) if length % k == 0)

        def step(i, carry):
            at = [i * group + k for k in range(group)]
            for k, result in [(k, value(k)) for k in at]:
                dst[k] = result
            return carry
        lax.fori_loop(0, length // group, step, 0)

    def clear(q, carry):
        @pl.when(jnp.logical_not(has_prev))
        def _():
            x0[q, pl.ds(0, HALO)] = jnp.zeros((HALO, around, depth), jnp.float32)

        @pl.when(jnp.logical_not(has_next))
        def _():
            x0[q, pl.ds(own + HALO, HALO)] = jnp.zeros((HALO, around, depth), jnp.float32)
        return carry

    def pass_on(q):
        here = x0.at[q, pl.ds(HALO, own)]
        pltpu.make_async_copy(here, here, recv1.at[q]).wait()
        halo(q, "start")

    def begin(q, carry):
        first_pass(q, "start")
        return carry

    first_pass(0, "start")
    speeds("start")
    lax.fori_loop(1, min(AHEAD, count) + 1, begin, 0)
    lax.fori_loop(0, count + 1, clear, 0)
    speeds("recv")
    pass_on(0)
    pass_on(1)
    lax.fori_loop(min(AHEAD, count) + 1, count + 1, begin, 0)
    speeds("load")
    halo(0, "recv")

    each_row(own + 2 * HALO, lambda i: x0[0, i] * (1.0 / 12.0), kap)

    def tick(t, carry):
        q = t
        f = q - 1
        halo(q, "recv")
        base = x0.at[q]

        def value1(i):
            u, change = operate(base, f, i, i + 2)
            return u + change
        each_row(own + 2 * HALO - 4, value1, x1)

        def value2(i):
            u, change = operate(x1, f, i, i + 4)
            half = 0.5 * (base[i + 4] + u + change)
            return pltpu.roll(half, of_row(turns, i + 4, 0), 0)
        each_row(own + 2 * HALO - 8, value2, x2)

        @pl.when(t < count)
        def _():
            pass_on(t + 1)

        def value3(i):
            u, change = operate(x2, f, i, i + 6)
            return u + change
        each_row(own + 2 * HALO - 12, value3, x3)

        def value4(i):
            u, change = operate(x3, f, i, i + 8)
            return 0.5 * (x2[i + 4] + u + change)
        each_row(own, value4, adv.at[f])
        second_pass(f, "start")
        return carry

    lax.fori_loop(1, count + 1, tick, 0)

    speeds("send")
    first_pass(0, "send")
    halo(0, "send")

    def finish(f, carry):
        first_pass(f + 1, "send")
        halo(f + 1, "send")
        second_pass(f, "send")
        pltpu.make_async_copy(out.at[f], out.at[f], recv2.at[f]).wait()
        return carry
    lax.fori_loop(0, count, finish, 0)


def shards(fields, kappa, radial_speed, azimuth_speed, shifts):
    n = lax.axis_size("azi")
    annuli = lax.axis_size("rad")
    count, rows, width, depth = fields.shape
    own, around = rows // n, width * n
    if own < HALO or n % 2:
        return shards_by_steps(fields, kappa, radial_speed, azimuth_speed, shifts)
    tall = own + 2 * HALO

    def scratch(*lead):
        return pltpu.VMEM((*lead, around, depth), jnp.float32)

    held = 4 * around * depth * ((count + 2) * tall + 3 * tall + count * own)
    any_space = pl.BlockSpec(memory_space=pl.ANY)
    table = radial_speed.shape
    dma = pltpu.SemaphoreType.DMA
    return pl.pallas_call(
        functools.partial(kernel, n, n * annuli),
        out_shape=jax.ShapeDtypeStruct(fields.shape, jnp.float32),
        in_specs=[any_space] * 5,
        out_specs=any_space,
        scratch_shapes=[
            scratch(count + 1, tall), scratch(tall - 4), scratch(tall - 8), scratch(tall - 12),
            scratch(count, own), scratch(tall),
            pltpu.VMEM((2, *table), jnp.float32), pltpu.VMEM((2, *table), jnp.float32),
            pltpu.VMEM((2, 1, rows), jnp.int32), pltpu.SMEM((3, *table), jnp.float32),
            pltpu.SMEM((3, *table), jnp.float32), pltpu.SMEM((3, 1, rows), jnp.int32),
            dma((3, 2)), dma((3, 2)), dma((3, 3)),
            dma((count + 1, n)), dma((count + 1,)), dma((count + 1,)), dma((count + 1,)),
            dma((count + 1, 2)), dma((count + 1, 2)), dma((count, n)), dma((count,)),
        ],
        compiler_params=pltpu.CompilerParams(
            collective_id=0, has_side_effects=True, vmem_limit_bytes=max(held + (8 << 20), 60 << 20)),
    )(radial_speed, azimuth_speed, shifts[None], fields, kappa)


def kernel_by_steps(n, blocks, srad, sazi, shifts, fields, kappa, out, x0, x1, x2, x3, adv, kap,
           send1, recv1, send_h, recv_h, send2, recv2):
    count, rows, width = fields.shape[0], fields.shape[1], fields.shape[2]
    own = rows // n
    around = width * n
    depth = fields.shape[3]
    rad, azi = lax.axis_index("rad"), lax.axis_index("azi")
    mine = block_of(rad, azi, n)
    home = mine // n
    spot = lax.rem(mine, n)
    has_prev, has_next = mine > 0, mine < blocks - 1
    prev = owner_of(jnp.maximum(mine - 1, 0), n)
    following = owner_of(jnp.minimum(mine + 1, blocks - 1), n)
    targets = [owner_of(rad * n + b, n) for b in range(n)]
    same = [jnp.logical_and(d[0] == rad, d[1] == azi) for d in targets]
    sources = [(home, jnp.int32(a)) for a in range(n)]
    back = [jnp.logical_and(home == rad, azi == a) for a in range(n)]

    barrier = pltpu.get_barrier_semaphore()
    greeted = jnp.int32(0)
    for device, skip in [*zip(targets, same), *zip(sources, back),
                         (prev, jnp.logical_not(has_prev)), (following, jnp.logical_not(has_next))]:
        @pl.when(jnp.logical_not(skip))
        def _():
            pl.semaphore_signal(barrier, inc=1, device_id=device, device_id_type=MESH)
        greeted = greeted + jnp.where(skip, 0, 1)
    pl.semaphore_wait(barrier, greeted)

    def first_pass(f, act):
        for b in range(n):
            def parts():
                at = pl.ds(azi * width, width)
                if f is None:
                    return kappa.at[pl.ds(b * own, own)], kap.at[:, at], count
                return fields.at[f, pl.ds(b * own, own)], x0.at[f, pl.ds(2, own), at], f

            @pl.when(jnp.logical_not(same[b]))
            def _():
                src, dst, k = parts()
                copy = pltpu.make_async_remote_copy(
                    src, dst, send1.at[k, b], recv1.at[k], device_id=targets[b], device_id_type=MESH)
                copy.start() if act == "start" else copy.wait_send()

            if act == "start":
                @pl.when(same[b])
                def _():
                    src, dst, k = parts()
                    pltpu.make_async_copy(src, dst, recv1.at[k]).start()

    def second_pass(f, act):
        for a in range(n):
            def parts():
                return adv.at[f, :, pl.ds(a * width, width)], out.at[f, pl.ds(spot * own, own)]

            @pl.when(jnp.logical_not(back[a]))
            def _():
                src, dst = parts()
                copy = pltpu.make_async_remote_copy(
                    src, dst, send2.at[f, a], recv2.at[f], device_id=sources[a], device_id_type=MESH)
                copy.start() if act == "start" else copy.wait_send()

            if act == "start":
                @pl.when(back[a])
                def _():
                    src, dst = parts()
                    pltpu.make_async_copy(src, dst, recv2.at[f]).start()

    def halo(x, f, level, act):
        low = pltpu.make_async_remote_copy(
            x.at[f, pl.ds(2, 2)], x.at[f, pl.ds(own + 2, 2)], send_h.at[f, level, 0],
            recv_h.at[f, level, 0], device_id=prev, device_id_type=MESH)
        high = pltpu.make_async_remote_copy(
            x.at[f, pl.ds(own, 2)], x.at[f, pl.ds(0, 2)], send_h.at[f, level, 1],
            recv_h.at[f, level, 1], device_id=following, device_id_type=MESH)

        @pl.when(has_prev)
        def _():
            if act == "start":
                low.start()
            elif act == "send":
                low.wait_send()
            else:
                high.wait_recv()

        @pl.when(has_next)
        def _():
            if act == "start":
                high.start()
            elif act == "send":
                high.wait_send()
            else:
                low.wait_recv()

    lane = lax.broadcasted_iota(jnp.int32, (around, depth), 1)

    def operate(x, f, i):
        u = x[f, i + 2]
        r2m, r1m, r1p, r2p = x[f, i], x[f, i + 1], x[f, i + 3], x[f, i + 4]
        p1p, p1m = pltpu.roll(u, around - 1, 0), pltpu.roll(u, 1, 0)
        p2p, p2m = pltpu.roll(u, around - 2, 0), pltpu.roll(u, 2, 0)
        z1p = jnp.where(lane < depth - 1, pltpu.roll(u, depth - 1, 1), 0.0)
        z1m = jnp.where(lane >= 1, pltpu.roll(u, 1, 1), 0.0)
        z2p = jnp.where(lane < depth - 2, pltpu.roll(u, depth - 2, 1), 0.0)
        z2m = jnp.where(lane >= 2, pltpu.roll(u, 2, 1), 0.0)
        one = (r1p + r1m) + (p1p + p1m) + (z1p + z1m)
        two = (r2p + r2m) + (p2p + p2m) + (z2p + z2m)
        spread = 16.0 * one - two - 90.0 * u
        carried = (srad[f, i] * (8.0 * (r1p - r1m) - (r2p - r2m))
                   + sazi[f, i] * (8.0 * (p1p - p1m) - (p2p - p2m)))
        return u, kap[i] * spread - carried

    def each_row(body):
        def step(i, carry):
            body(i)
            return carry
        lax.fori_loop(0, own, step, 0)

    def clear(f, carry):
        for x in (x0, x1, x2, x3):
            @pl.when(jnp.logical_not(has_prev))
            def _():
                x[f, pl.ds(0, 2)] = jnp.zeros((2, around, depth), jnp.float32)

            @pl.when(jnp.logical_not(has_next))
            def _():
                x[f, pl.ds(own + 2, 2)] = jnp.zeros((2, around, depth), jnp.float32)
        return carry

    first_pass(0, "start")
    first_pass(None, "start")
    for f in range(1, min(AHEAD, count)):
        first_pass(f, "start")
    lax.fori_loop(0, count, clear, 0)
    pltpu.make_async_copy(kap, kap, recv1.at[count]).wait()

    def scale(i):
        kap[i] = kap[i] * (1.0 / 12.0)
    each_row(scale)

    def tick(t, carry):
        def at_stage(lag):
            f = t - lag
            return f, jnp.logical_and(f >= 0, f < count)

        f_next, fine = at_stage(-AHEAD)

        @pl.when(fine)
        def _():
            first_pass(f_next, "start")

        f4, fine4 = at_stage(4)

        @pl.when(fine4)
        def _():
            halo(x3, f4, 3, "recv")

            def body(i):
                u, change = operate(x3, f4, i)
                adv[f4, i] = 0.5 * (x2[f4, i + 2] + u + change)
            each_row(body)
            second_pass(f4, "start")

        f3, fine3 = at_stage(3)

        @pl.when(fine3)
        def _():
            halo(x2, f3, 2, "recv")

            def body(i):
                u, change = operate(x2, f3, i)
                x3[f3, i + 2] = u + change
            each_row(body)
            halo(x3, f3, 3, "start")

        f2, fine2 = at_stage(2)

        @pl.when(fine2)
        def _():
            halo(x1, f2, 1, "recv")

            def body(i):
                u, change = operate(x1, f2, i)
                half = 0.5 * (x0[f2, i + 2] + u + change)
                x2[f2, i + 2] = pltpu.roll(half, shifts[i], 0)
            each_row(body)
            halo(x2, f2, 2, "start")

        f1, fine1 = at_stage(1)

        @pl.when(fine1)
        def _():
            halo(x0, f1, 0, "recv")

            def body(i):
                u, change = operate(x0, f1, i)
                x1[f1, i + 2] = u + change
            each_row(body)
            halo(x1, f1, 1, "start")

        f0, fine0 = at_stage(0)

        @pl.when(fine0)
        def _():
            here = x0.at[f0, pl.ds(2, own)]
            pltpu.make_async_copy(here, here, recv1.at[f0]).wait()
            halo(x0, f0, 0, "start")
        return carry

    lax.fori_loop(0, count + STAGES, tick, 0)

    first_pass(None, "send")

    def finish(f, carry):
        first_pass(f, "send")
        for level, x in enumerate((x0, x1, x2, x3)):
            halo(x, f, level, "send")
        second_pass(f, "send")
        pltpu.make_async_copy(out.at[f], out.at[f], recv2.at[f]).wait()
        return carry
    lax.fori_loop(0, count, finish, 0)


def shards_by_steps(fields, kappa, radial_speed, azimuth_speed, shifts):
    n = lax.axis_size("azi")
    annuli = lax.axis_size("rad")
    count, rows, width, depth = fields.shape
    own, around = rows // n, width * n
    rad, azi = lax.axis_index("rad"), lax.axis_index("azi")
    mine = block_of(rad, azi, n)
    packed = jnp.concatenate(
        [radial_speed * (1.0 / 12.0), azimuth_speed * (1.0 / 12.0),
         jnp.mod(shifts, around).astype(jnp.float32)[None]], axis=0)
    other = lax.ppermute(packed, "rad", [(i, i ^ 1) for i in range(annuli)])
    rightful = jnp.where(mine // n == rad, packed, other)
    rightful = lax.dynamic_slice_in_dim(rightful, (mine % n) * own, own, axis=1)
    srad, sazi = rightful[:count], rightful[count:2 * count]
    turn = rightful[2 * count].astype(jnp.int32)

    tall = pltpu.VMEM((count, own + 4, around, depth), jnp.float32)
    held = 4 * count * around * depth * (4 * (own + 4) + own + own)
    any_space = pl.BlockSpec(memory_space=pl.ANY)
    small = pl.BlockSpec(memory_space=pltpu.SMEM)
    return pl.pallas_call(
        functools.partial(kernel_by_steps, n, n * annuli),
        out_shape=jax.ShapeDtypeStruct(fields.shape, jnp.float32),
        in_specs=[small, small, small, any_space, any_space],
        out_specs=any_space,
        scratch_shapes=[
            tall, tall, tall, tall,
            pltpu.VMEM((count, own, around, depth), jnp.float32),
            pltpu.VMEM((own, around, depth), jnp.float32),
            pltpu.SemaphoreType.DMA((count + 1, n)),
            pltpu.SemaphoreType.DMA((count + 1,)),
            pltpu.SemaphoreType.DMA((count, STAGES, 2)),
            pltpu.SemaphoreType.DMA((count, STAGES, 2)),
            pltpu.SemaphoreType.DMA((count, n)),
            pltpu.SemaphoreType.DMA((count,)),
        ],
        compiler_params=pltpu.CompilerParams(
            collective_id=1, has_side_effects=True, vmem_limit_bytes=held + (8 << 20)),
    )(srad, sazi, turn, fields, kappa)


def solution(mesh):
    placed = (
        P(None, "rad", "azi", None),
        P("rad", "azi", None),
        P(None, "rad"),
        P(None, "rad"),
        P("rad"),
    )
    return jax.shard_map(
        shards, mesh=mesh, in_specs=placed, out_specs=P(None, "rad", "azi", None), check_vma=False
    )
```

```python
import functools

import jax
import jax.numpy as jnp
from jax import lax
from jax.experimental import pallas as pl
from jax.experimental.pallas import tpu as pltpu
from jax.sharding import PartitionSpec as P

MESH = pl.DeviceIdType.MESH
HALO = 8
STAGES = 4
AHEAD = 2
GROUP = 4


def block_of(rad, azi, n):
    column = rad // 2
    odd = lax.rem(column, 2)
    place = azi + odd * (n - 1 - 2 * azi)
    return column * (2 * n) + 2 * place + lax.rem(rad, 2)


def owner_of(block, n):
    column = block // (2 * n)
    t = lax.rem(block, 2 * n)
    odd = lax.rem(column, 2)
    place = t // 2
    return 2 * column + lax.rem(t, 2), place + odd * (n - 1 - 2 * place)


def kernel(n, blocks, fast_r, fast_p, shifts, fields, kappa, out, x0, x1, x2, x3, adv, kap,
           near_r, near_p, near_s, srad, sazi, turns, send_n, recv_n, load_n, send1, recv1, send_x, recv_x, send_h, recv_h, send2, recv2):
    count, rows, width, depth = fields.shape
    own = rows // n
    around = width * n
    rad, azi = lax.axis_index("rad"), lax.axis_index("azi")
    core = lax.rem(rad, 2)
    mine = block_of(rad, azi, n)
    home = mine // n
    spot = lax.rem(mine, n)
    turn = lax.rem(mine, 2 * n)
    middle = jnp.logical_or(turn == n, turn == n - 1)
    has_prev, has_next = mine > 0, mine < blocks - 1
    from_prev = jnp.logical_and(has_prev, turn != n)
    from_next = jnp.logical_and(has_next, turn != n - 1)
    prev = owner_of(jnp.maximum(mine - 1, 0), n)
    following = owner_of(jnp.minimum(mine + 1, blocks - 1), n)

    def is_me(device):
        return jnp.logical_and(device[0] == rad, device[1] == azi)

    targets = [owner_of(rad * n + b, n) for b in range(n)]
    same = [is_me(d) for d in targets]
    sources = [(home, jnp.int32(a)) for a in range(n)]
    back = [is_me(d) for d in sources]
    across = owner_of(rad * n + n - core * (n + 1), n)
    across_same = is_me(across)
    holders = [(home + 1 - 2 * lax.rem(home, 2), jnp.int32(a)) for a in range(n)]
    not_held = [jnp.logical_or(jnp.logical_not(middle), is_me(d)) for d in holders]

    below_in, above_in = rad > 0, rad < blocks // n - 1
    below = (jnp.maximum(rad - 1, 0), azi)
    above = (jnp.minimum(rad + 1, blocks // n - 1), azi)

    barrier = pltpu.get_barrier_semaphore()
    greeted = jnp.int32(0)
    for device, skip in [*zip(targets, same), *zip(sources, back), (across, across_same),
                         *zip(holders, not_held), (prev, jnp.logical_not(from_prev)),
                         (below, jnp.logical_not(below_in)), (above, jnp.logical_not(above_in)),
                         (following, jnp.logical_not(from_next))]:
        @pl.when(jnp.logical_not(skip))
        def _():
            pl.semaphore_signal(barrier, inc=1, device_id=device, device_id_type=MESH)
        greeted = greeted + jnp.where(skip, 0, 1)
    pl.semaphore_wait(barrier, greeted)

    def move(act, src, dst, send, recv, device, local):
        @pl.when(jnp.logical_not(local))
        def _():
            copy = pltpu.make_async_remote_copy(
                src, dst, send, recv, device_id=device, device_id_type=MESH)
            copy.start() if act == "start" else copy.wait_send()

        if act == "start":
            @pl.when(local)
            def _():
                pltpu.make_async_copy(src, dst, recv).start()

    def held(q):
        return kappa if isinstance(q, int) else fields.at[q - 1]

    def first_pass(q, act):
        at = pl.ds(azi * width, width)
        edge = (1 - core) * (rows - HALO)
        move(act, held(q).at[pl.ds(edge, HALO)], x0.at[q, pl.ds(core * (HALO + own), HALO), at],
             send_x.at[q], recv_x.at[q], across, across_same)
        for b in range(n):
            move(act, held(q).at[pl.ds(b * own, own)], x0.at[q, pl.ds(HALO, own), at],
                 send1.at[q, b], recv1.at[q], targets[b], same[b])

    def second_pass(f, act):
        for a in range(n):
            move(act, adv.at[f, :, pl.ds(a * width, width)], out.at[f, pl.ds(spot * own, own)],
                 send2.at[f, a], recv2.at[f], sources[a], back[a])

    def halo(q, act):
        low = pltpu.make_async_remote_copy(
            x0.at[q, pl.ds(HALO, HALO)], x0.at[q, pl.ds(own + HALO, HALO)], send_h.at[q, 0],
            recv_h.at[q, 0], device_id=prev, device_id_type=MESH)
        high = pltpu.make_async_remote_copy(
            x0.at[q, pl.ds(own, HALO)], x0.at[q, pl.ds(0, HALO)], send_h.at[q, 1],
            recv_h.at[q, 1], device_id=following, device_id_type=MESH)

        @pl.when(from_prev)
        def _():
            if act == "start":
                low.start()
            elif act == "send":
                low.wait_send()
            else:
                high.wait_recv()

        @pl.when(from_next)
        def _():
            if act == "start":
                high.start()
            elif act == "send":
                high.wait_send()
            else:
                low.wait_recv()

        if act == "recv":
            @pl.when(middle)
            def _():
                here = x0.at[q, pl.ds(0, HALO)]
                pltpu.make_async_copy(here, here, recv_x.at[q]).wait()

    small = ((fast_r, near_r, srad), (fast_p, near_p, sazi), (shifts, near_s, turns))

    def speeds(act):
        for k, (mine_k, near, held_k) in enumerate(small):
            for side, device, there in ((0, below, below_in), (1, above, above_in)):
                slot = 1 - side
                copy = pltpu.make_async_remote_copy(
                    mine_k, near.at[slot], send_n.at[k, side], recv_n.at[k, slot],
                    device_id=device, device_id_type=MESH)
                arrived = pltpu.make_async_remote_copy(
                    mine_k, near.at[side], send_n.at[k, slot], recv_n.at[k, side],
                    device_id=device, device_id_type=MESH)
                inward = pltpu.make_async_copy(
                    near.at[side], held_k.at[2 * side], load_n.at[k, side])

                @pl.when(there)
                def _():
                    if act == "start":
                        copy.start()
                    elif act == "send":
                        copy.wait_send()
                    elif act == "recv":
                        arrived.wait_recv()
                        inward.start()
                    else:
                        inward.wait()
            own_copy = pltpu.make_async_copy(mine_k, held_k.at[1], load_n.at[k, 2])
            if act == "start":
                own_copy.start()
            elif act == "load":
                own_copy.wait()

    first_row = mine * own - HALO
    total_rows = blocks * own

    def of_row(table, row, *lead):
        at = first_row + row
        inside = jnp.logical_and(at >= 0, at < total_rows)
        at = jnp.clip(at, 0, total_rows - 1) - (rad - 1) * rows
        return jnp.where(inside, table[(at // rows, *lead, lax.rem(at, rows))], 0)

    lane = lax.broadcasted_iota(jnp.int32, (around, depth), 1)

    def operate(x, f, i, row):
        u = x[i + 2]
        r2m, r1m, r1p, r2p = x[i], x[i + 1], x[i + 3], x[i + 4]
        p1p, p1m = pltpu.roll(u, around - 1, 0), pltpu.roll(u, 1, 0)
        p2p, p2m = pltpu.roll(u, around - 2, 0), pltpu.roll(u, 2, 0)
        z1p = jnp.where(lane < depth - 1, pltpu.roll(u, depth - 1, 1), 0.0)
        z1m = jnp.where(lane >= 1, pltpu.roll(u, 1, 1), 0.0)
        z2p = jnp.where(lane < depth - 2, pltpu.roll(u, depth - 2, 1), 0.0)
        z2m = jnp.where(lane >= 2, pltpu.roll(u, 2, 1), 0.0)
        one = (r1p + r1m) + (p1p + p1m) + (z1p + z1m)
        two = (r2p + r2m) + (p2p + p2m) + (z2p + z2m)
        spread = 16.0 * one - two - 90.0 * u
        fast = of_row(srad, row, f) * (1.0 / 12.0)
        slow = of_row(sazi, row, f) * (1.0 / 12.0)
        carried = (fast * (8.0 * (r1p - r1m) - (r2p - r2m))
                   + slow * (8.0 * (p1p - p1m) - (p2p - p2m)))
        return u, kap[row] * spread - carried

    def each_row(length, value, dst):
        group = next(k for k in (GROUP, 2, 1) if length % k == 0)

        def step(i, carry):
            at = [i * group + k for k in range(group)]
            for k, result in [(k, value(k)) for k in at]:
                dst[k] = result
            return carry
        lax.fori_loop(0, length // group, step, 0)

    def clear(q, carry):
        @pl.when(jnp.logical_not(has_prev))
        def _():
            x0[q, pl.ds(0, HALO)] = jnp.zeros((HALO, around, depth), jnp.float32)

        @pl.when(jnp.logical_not(has_next))
        def _():
            x0[q, pl.ds(own + HALO, HALO)] = jnp.zeros((HALO, around, depth), jnp.float32)
        return carry

    def pass_on(q):
        here = x0.at[q, pl.ds(HALO, own)]
        pltpu.make_async_copy(here, here, recv1.at[q]).wait()
        halo(q, "start")

    def begin(q, carry):
        first_pass(q, "start")
        return carry

    first_pass(0, "start")
    speeds("start")
    lax.fori_loop(1, min(AHEAD, count) + 1, begin, 0)
    lax.fori_loop(0, count + 1, clear, 0)
    speeds("recv")
    pass_on(0)
    pass_on(1)
    speeds("load")
    halo(0, "recv")

    each_row(own + 2 * HALO, lambda i: x0[0, i] * (1.0 / 12.0), kap)

    def tick(t, carry):
        @pl.when(t + AHEAD <= count)
        def _():
            first_pass(t + AHEAD, "start")

        q = t
        f = q - 1
        halo(q, "recv")
        base = x0.at[q]

        def value1(i):
            u, change = operate(base, f, i, i + 2)
            return u + change
        each_row(own + 2 * HALO - 4, value1, x1)

        def value2(i):
            u, change = operate(x1, f, i, i + 4)
            half = 0.5 * (base[i + 4] + u + change)
            return pltpu.roll(half, of_row(turns, i + 4, 0), 0)
        each_row(own + 2 * HALO - 8, value2, x2)

        @pl.when(t < count)
        def _():
            pass_on(t + 1)

        def value3(i):
            u, change = operate(x2, f, i, i + 6)
            return u + change
        each_row(own + 2 * HALO - 12, value3, x3)

        def value4(i):
            u, change = operate(x3, f, i, i + 8)
            return 0.5 * (x2[i + 4] + u + change)
        each_row(own, value4, adv.at[f])
        second_pass(f, "start")
        return carry

    lax.fori_loop(1, count + 1, tick, 0)

    speeds("send")
    first_pass(0, "send")
    halo(0, "send")

    def finish(f, carry):
        first_pass(f + 1, "send")
        halo(f + 1, "send")
        second_pass(f, "send")
        pltpu.make_async_copy(out.at[f], out.at[f], recv2.at[f]).wait()
        return carry
    lax.fori_loop(0, count, finish, 0)


def shards(fields, kappa, radial_speed, azimuth_speed, shifts):
    n = lax.axis_size("azi")
    annuli = lax.axis_size("rad")
    count, rows, width, depth = fields.shape
    own, around = rows // n, width * n
    if own < HALO or n % 2:
        return shards_by_steps(fields, kappa, radial_speed, azimuth_speed, shifts)
    tall = own + 2 * HALO

    def scratch(*lead):
        return pltpu.VMEM((*lead, around, depth), jnp.float32)

    held = 4 * around * depth * ((count + 2) * tall + 3 * tall + count * own)
    any_space = pl.BlockSpec(memory_space=pl.ANY)
    table = radial_speed.shape
    dma = pltpu.SemaphoreType.DMA
    return pl.pallas_call(
        functools.partial(kernel, n, n * annuli),
        out_shape=jax.ShapeDtypeStruct(fields.shape, jnp.float32),
        in_specs=[any_space] * 5,
        out_specs=any_space,
        scratch_shapes=[
            scratch(count + 1, tall), scratch(tall - 4), scratch(tall - 8), scratch(tall - 12),
            scratch(count, own), scratch(tall),
            pltpu.VMEM((2, *table), jnp.float32), pltpu.VMEM((2, *table), jnp.float32),
            pltpu.VMEM((2, 1, rows), jnp.int32), pltpu.SMEM((3, *table), jnp.float32),
            pltpu.SMEM((3, *table), jnp.float32), pltpu.SMEM((3, 1, rows), jnp.int32),
            dma((3, 2)), dma((3, 2)), dma((3, 3)),
            dma((count + 1, n)), dma((count + 1,)), dma((count + 1,)), dma((count + 1,)),
            dma((count + 1, 2)), dma((count + 1, 2)), dma((count, n)), dma((count,)),
        ],
        compiler_params=pltpu.CompilerParams(
            collective_id=0, has_side_effects=True, vmem_limit_bytes=max(held + (8 << 20), 60 << 20)),
    )(radial_speed, azimuth_speed, shifts[None], fields, kappa)


def kernel_by_steps(n, blocks, srad, sazi, shifts, fields, kappa, out, x0, x1, x2, x3, adv, kap,
           send1, recv1, send_h, recv_h, send2, recv2):
    count, rows, width = fields.shape[0], fields.shape[1], fields.shape[2]
    own = rows // n
    around = width * n
    depth = fields.shape[3]
    rad, azi = lax.axis_index("rad"), lax.axis_index("azi")
    mine = block_of(rad, azi, n)
    home = mine // n
    spot = lax.rem(mine, n)
    has_prev, has_next = mine > 0, mine < blocks - 1
    prev = owner_of(jnp.maximum(mine - 1, 0), n)
    following = owner_of(jnp.minimum(mine + 1, blocks - 1), n)
    targets = [owner_of(rad * n + b, n) for b in range(n)]
    same = [jnp.logical_and(d[0] == rad, d[1] == azi) for d in targets]
    sources = [(home, jnp.int32(a)) for a in range(n)]
    back = [jnp.logical_and(home == rad, azi == a) for a in range(n)]

    barrier = pltpu.get_barrier_semaphore()
    greeted = jnp.int32(0)
    for device, skip in [*zip(targets, same), *zip(sources, back),
                         (prev, jnp.logical_not(has_prev)), (following, jnp.logical_not(has_next))]:
        @pl.when(jnp.logical_not(skip))
        def _():
            pl.semaphore_signal(barrier, inc=1, device_id=device, device_id_type=MESH)
        greeted = greeted + jnp.where(skip, 0, 1)
    pl.semaphore_wait(barrier, greeted)

    def first_pass(f, act):
        for b in range(n):
            def parts():
                at = pl.ds(azi * width, width)
                if f is None:
                    return kappa.at[pl.ds(b * own, own)], kap.at[:, at], count
                return fields.at[f, pl.ds(b * own, own)], x0.at[f, pl.ds(2, own), at], f

            @pl.when(jnp.logical_not(same[b]))
            def _():
                src, dst, k = parts()
                copy = pltpu.make_async_remote_copy(
                    src, dst, send1.at[k, b], recv1.at[k], device_id=targets[b], device_id_type=MESH)
                copy.start() if act == "start" else copy.wait_send()

            if act == "start":
                @pl.when(same[b])
                def _():
                    src, dst, k = parts()
                    pltpu.make_async_copy(src, dst, recv1.at[k]).start()

    def second_pass(f, act):
        for a in range(n):
            def parts():
                return adv.at[f, :, pl.ds(a * width, width)], out.at[f, pl.ds(spot * own, own)]

            @pl.when(jnp.logical_not(back[a]))
            def _():
                src, dst = parts()
                copy = pltpu.make_async_remote_copy(
                    src, dst, send2.at[f, a], recv2.at[f], device_id=sources[a], device_id_type=MESH)
                copy.start() if act == "start" else copy.wait_send()

            if act == "start":
                @pl.when(back[a])
                def _():
                    src, dst = parts()
                    pltpu.make_async_copy(src, dst, recv2.at[f]).start()

    def halo(x, f, level, act):
        low = pltpu.make_async_remote_copy(
            x.at[f, pl.ds(2, 2)], x.at[f, pl.ds(own + 2, 2)], send_h.at[f, level, 0],
            recv_h.at[f, level, 0], device_id=prev, device_id_type=MESH)
        high = pltpu.make_async_remote_copy(
            x.at[f, pl.ds(own, 2)], x.at[f, pl.ds(0, 2)], send_h.at[f, level, 1],
            recv_h.at[f, level, 1], device_id=following, device_id_type=MESH)

        @pl.when(has_prev)
        def _():
            if act == "start":
                low.start()
            elif act == "send":
                low.wait_send()
            else:
                high.wait_recv()

        @pl.when(has_next)
        def _():
            if act == "start":
                high.start()
            elif act == "send":
                high.wait_send()
            else:
                low.wait_recv()

    lane = lax.broadcasted_iota(jnp.int32, (around, depth), 1)

    def operate(x, f, i):
        u = x[f, i + 2]
        r2m, r1m, r1p, r2p = x[f, i], x[f, i + 1], x[f, i + 3], x[f, i + 4]
        p1p, p1m = pltpu.roll(u, around - 1, 0), pltpu.roll(u, 1, 0)
        p2p, p2m = pltpu.roll(u, around - 2, 0), pltpu.roll(u, 2, 0)
        z1p = jnp.where(lane < depth - 1, pltpu.roll(u, depth - 1, 1), 0.0)
        z1m = jnp.where(lane >= 1, pltpu.roll(u, 1, 1), 0.0)
        z2p = jnp.where(lane < depth - 2, pltpu.roll(u, depth - 2, 1), 0.0)
        z2m = jnp.where(lane >= 2, pltpu.roll(u, 2, 1), 0.0)
        one = (r1p + r1m) + (p1p + p1m) + (z1p + z1m)
        two = (r2p + r2m) + (p2p + p2m) + (z2p + z2m)
        spread = 16.0 * one - two - 90.0 * u
        carried = (srad[f, i] * (8.0 * (r1p - r1m) - (r2p - r2m))
                   + sazi[f, i] * (8.0 * (p1p - p1m) - (p2p - p2m)))
        return u, kap[i] * spread - carried

    def each_row(body):
        def step(i, carry):
            body(i)
            return carry
        lax.fori_loop(0, own, step, 0)

    def clear(f, carry):
        for x in (x0, x1, x2, x3):
            @pl.when(jnp.logical_not(has_prev))
            def _():
                x[f, pl.ds(0, 2)] = jnp.zeros((2, around, depth), jnp.float32)

            @pl.when(jnp.logical_not(has_next))
            def _():
                x[f, pl.ds(own + 2, 2)] = jnp.zeros((2, around, depth), jnp.float32)
        return carry

    first_pass(0, "start")
    first_pass(None, "start")
    for f in range(1, min(AHEAD, count)):
        first_pass(f, "start")
    lax.fori_loop(0, count, clear, 0)
    pltpu.make_async_copy(kap, kap, recv1.at[count]).wait()

    def scale(i):
        kap[i] = kap[i] * (1.0 / 12.0)
    each_row(scale)

    def tick(t, carry):
        def at_stage(lag):
            f = t - lag
            return f, jnp.logical_and(f >= 0, f < count)

        f_next, fine = at_stage(-AHEAD)

        @pl.when(fine)
        def _():
            first_pass(f_next, "start")

        f4, fine4 = at_stage(4)

        @pl.when(fine4)
        def _():
            halo(x3, f4, 3, "recv")

            def body(i):
                u, change = operate(x3, f4, i)
                adv[f4, i] = 0.5 * (x2[f4, i + 2] + u + change)
            each_row(body)
            second_pass(f4, "start")

        f3, fine3 = at_stage(3)

        @pl.when(fine3)
        def _():
            halo(x2, f3, 2, "recv")

            def body(i):
                u, change = operate(x2, f3, i)
                x3[f3, i + 2] = u + change
            each_row(body)
            halo(x3, f3, 3, "start")

        f2, fine2 = at_stage(2)

        @pl.when(fine2)
        def _():
            halo(x1, f2, 1, "recv")

            def body(i):
                u, change = operate(x1, f2, i)
                half = 0.5 * (x0[f2, i + 2] + u + change)
                x2[f2, i + 2] = pltpu.roll(half, shifts[i], 0)
            each_row(body)
            halo(x2, f2, 2, "start")

        f1, fine1 = at_stage(1)

        @pl.when(fine1)
        def _():
            halo(x0, f1, 0, "recv")

            def body(i):
                u, change = operate(x0, f1, i)
                x1[f1, i + 2] = u + change
            each_row(body)
            halo(x1, f1, 1, "start")

        f0, fine0 = at_stage(0)

        @pl.when(fine0)
        def _():
            here = x0.at[f0, pl.ds(2, own)]
            pltpu.make_async_copy(here, here, recv1.at[f0]).wait()
            halo(x0, f0, 0, "start")
        return carry

    lax.fori_loop(0, count + STAGES, tick, 0)

    first_pass(None, "send")

    def finish(f, carry):
        first_pass(f, "send")
        for level, x in enumerate((x0, x1, x2, x3)):
            halo(x, f, level, "send")
        second_pass(f, "send")
        pltpu.make_async_copy(out.at[f], out.at[f], recv2.at[f]).wait()
        return carry
    lax.fori_loop(0, count, finish, 0)


def shards_by_steps(fields, kappa, radial_speed, azimuth_speed, shifts):
    n = lax.axis_size("azi")
    annuli = lax.axis_size("rad")
    count, rows, width, depth = fields.shape
    own, around = rows // n, width * n
    rad, azi = lax.axis_index("rad"), lax.axis_index("azi")
    mine = block_of(rad, azi, n)
    packed = jnp.concatenate(
        [radial_speed * (1.0 / 12.0), azimuth_speed * (1.0 / 12.0),
         jnp.mod(shifts, around).astype(jnp.float32)[None]], axis=0)
    other = lax.ppermute(packed, "rad", [(i, i ^ 1) for i in range(annuli)])
    rightful = jnp.where(mine // n == rad, packed, other)
    rightful = lax.dynamic_slice_in_dim(rightful, (mine % n) * own, own, axis=1)
    srad, sazi = rightful[:count], rightful[count:2 * count]
    turn = rightful[2 * count].astype(jnp.int32)

    tall = pltpu.VMEM((count, own + 4, around, depth), jnp.float32)
    held = 4 * count * around * depth * (4 * (own + 4) + own + own)
    any_space = pl.BlockSpec(memory_space=pl.ANY)
    small = pl.BlockSpec(memory_space=pltpu.SMEM)
    return pl.pallas_call(
        functools.partial(kernel_by_steps, n, n * annuli),
        out_shape=jax.ShapeDtypeStruct(fields.shape, jnp.float32),
        in_specs=[small, small, small, any_space, any_space],
        out_specs=any_space,
        scratch_shapes=[
            tall, tall, tall, tall,
            pltpu.VMEM((count, own, around, depth), jnp.float32),
            pltpu.VMEM((own, around, depth), jnp.float32),
            pltpu.SemaphoreType.DMA((count + 1, n)),
            pltpu.SemaphoreType.DMA((count + 1,)),
            pltpu.SemaphoreType.DMA((count, STAGES, 2)),
            pltpu.SemaphoreType.DMA((count, STAGES, 2)),
            pltpu.SemaphoreType.DMA((count, n)),
            pltpu.SemaphoreType.DMA((count,)),
        ],
        compiler_params=pltpu.CompilerParams(
            collective_id=1, has_side_effects=True, vmem_limit_bytes=held + (8 << 20)),
    )(srad, sazi, turn, fields, kappa)


def solution(mesh):
    placed = (
        P(None, "rad", "azi", None),
        P("rad", "azi", None),
        P(None, "rad"),
        P(None, "rad"),
        P("rad"),
    )
    return jax.shard_map(
        shards, mesh=mesh, in_specs=placed, out_specs=P(None, "rad", "azi", None), check_vma=False
    )
```
